256 devices in a mesh: ctx: 32 (over y, x, core), qry: 8 (over z).
Axes of the slice: x: 4, y: 4, z: 8, core: 2. Of those that a mesh axis runs over, the one named last changes fastest.
Arguments:
- idx_query: bfloat16 [256, 8192], P('ctx', 'qry'), may hold values from -200 to 200
- idx_weight: bfloat16 [256, 64], P('ctx', 'qry'), may hold values from -3 to 3
- idx_keys: bfloat16 [65536, 128], P('ctx'), may hold values from -6 to 6
- q_latent: bfloat16 [256, 73728], P(('ctx', 'qry')), may hold values from -400 to 400
- latent_cache: bfloat16 [65536, 576], P('ctx'), may hold values from -20 to 20
- page_ids: int32 [256, 32], P(('ctx', 'qry')), may hold values from 0 to 1023, as said below
Outputs:
- index_logp: float32 [256, 65536], P(('ctx', 'qry'))
- latent_out: bfloat16 [256, 65536], P(('ctx', 'qry'))
The draws below stay inside these ranges and needn't reach their ends.
Inputs may be any that keep to these rules, and one draw needn't show every extreme that they name: `page_ids`: each row names 32 distinct pages, and no page id appears twice in the 1 row of one device (aligned blocks of 1 row). Page p holds tokens p * 64 to p * 64 + 63; ctx index j holds pages j * 32 to (j + 1) * 32 - 1. Of the 32 ids in the rows of one device, at most 2 lie on one ctx index, and in every such block some ctx index holds exactly 2.
All inputs are finite; a program needn't handle non-finite values.
Results may differ from the reference program's by a relative error of at most 0.013.
Values may be sent and summed in bfloat16 or wider, within the bound.
No kernel may reach another device: no remote copies, remote signals or barrier semaphores. Data moves between devices by JAX's collectives and lax.ppermute only.
A program may use at most 64 MiB of HBM per device.

```python
import math
import jax
import jax.numpy as jnp
from jax import lax

H_IDX = 64
D_IDX = 128
H = 128
D_LAT = 512
D_ROPE = 64
QK_NOPE = 128
DK = 576
PAGE = 64
TOPP = 32
CTX_DEV = 2048
QR_DEV = 1
MOST = 2
PAGES_DEV = 32
PAGES = 1024
CTX = 65536
QROWS = 256


def draw_idx_query(key, part):
    norm_key = jax.random.fold_in(jax.random.fold_in(key, 11), 0)
    values = jnp.clip(jax.random.normal(norm_key, (QROWS, H_IDX * D_IDX), jnp.float32), -6.0, 6.0)
    return jnp.clip(values, -200.0, 200.0).astype(jnp.bfloat16)


def draw_idx_keys(key, part):
    norm_key = jax.random.fold_in(jax.random.fold_in(key, 13), 0)
    values = jnp.clip(jax.random.normal(norm_key, (CTX, D_IDX), jnp.float32), -6.0, 6.0) / math.sqrt(D_IDX)
    return jnp.clip(values, -6.0, 6.0).astype(jnp.bfloat16)


def draw_q_latent(key, part):
    norm_key = jax.random.fold_in(jax.random.fold_in(key, 17), 0)
    values = jnp.clip(jax.random.normal(norm_key, (QROWS, H, DK), jnp.float32), -6.0, 6.0)
    return jnp.clip(values, -400.0, 400.0).reshape(QROWS, H * DK).astype(jnp.bfloat16)


def draw_latent_cache(key, part):
    norm_key = jax.random.fold_in(jax.random.fold_in(key, 19), 0)
    values = jnp.clip(jax.random.normal(norm_key, (CTX, DK), jnp.float32), -6.0, 6.0)
    return jnp.clip(values, -20.0, 20.0).astype(jnp.bfloat16)


def draw_page_ids(key, part):
    shard_count = PAGES // PAGES_DEV
    wanted = QR_DEV * TOPP
    couple_count = shard_count * MOST
    heat_key, block_key = jax.random.split(jax.random.fold_in(key, 23))
    partition_load = jax.random.randint(heat_key, (shard_count,), 0, 4)
    couple_holder = jnp.arange(couple_count, dtype=jnp.int32) // MOST
    pair_copy = jnp.arange(couple_count, dtype=jnp.int32) % MOST

    def one_block(block_seed):
        seeds = jax.random.split(block_seed, 4)
        random_noise = jax.random.randint(seeds[0], (couple_count,), 0, 65536)
        compelled_pick = jax.random.randint(seeds[1], (), 0, shard_count)
        compelled_reward = jnp.where(couple_holder == compelled_pick, 1048576, 0)
        couple_score = (random_noise + partition_load[couple_holder] * 32768 + compelled_reward) * couple_count + jnp.arange(couple_count, dtype=jnp.int32)
        picked = lax.top_k(couple_score, wanted)[1]
        offset = jax.random.randint(seeds[2], (shard_count,), 0, PAGES_DEV)
        owner_shard = couple_holder[picked]
        local_page = (offset[owner_shard] + pair_copy[picked]) % PAGES_DEV
        page_list = owner_shard * PAGES_DEV + local_page
        shuffled = jax.random.permutation(seeds[3], page_list)
        return shuffled.reshape(QR_DEV, TOPP)
    block_seeds = jax.random.split(block_key, QROWS // QR_DEV)
    return jax.vmap(one_block)(block_seeds).reshape(QROWS, TOPP).astype(jnp.int32)


def block_scale(rng, dims, cuts, low, high):
    level, own = 1.0, jax.random.fold_in(rng, 6)
    for position, blocks in cuts:
        heights = jnp.exp(jax.random.uniform(jax.random.fold_in(own, position), (blocks,), jnp.float32, low / len(cuts), high / len(cuts)))
        level = level * jnp.repeat(heights, dims[position] // blocks).reshape([-1 if axis == position else 1 for axis in range(len(dims))])
    return level


def normal_values(key, dims, scale, most, cuts=(), kind=jnp.bfloat16):
    gain = block_scale(key, dims, cuts, -0.22, 0.18) if cuts else 1.0
    values = jax.random.normal(key, dims, jnp.float32) * scale * gain
    return jnp.minimum(jnp.maximum(values, -most), most).astype(kind)


def setup_inputs(seed: int = 0) -> dict:
    key_of = jax.random.split(jax.random.key(seed), 7)
    idx_query = draw_idx_query(jax.random.fold_in(key_of[6], 71), 0)
    idx_weight = normal_values(key_of[1], (QROWS, H_IDX), 0.7, 3.0, ((0, 32), (1, 8)))
    idx_keys = draw_idx_keys(jax.random.fold_in(key_of[6], 71), 0)
    q_latent = draw_q_latent(jax.random.fold_in(key_of[6], 71), 0)
    latent_cache = draw_latent_cache(jax.random.fold_in(key_of[6], 71), 0)
    page_ids = draw_page_ids(jax.random.fold_in(key_of[6], 71), 0)
    return dict(idx_query=idx_query, idx_weight=idx_weight, idx_keys=idx_keys, q_latent=q_latent, latent_cache=latent_cache, page_ids=page_ids)


def reference(idx_query, idx_weight, idx_keys, q_latent, latent_cache, page_ids):
    block_width = min(512, CTX_DEV)
    query_flat = idx_query.astype(jnp.float32).reshape(QROWS * H_IDX, D_IDX)
    head_weights = idx_weight.astype(jnp.float32)
    key_blocks = idx_keys.astype(jnp.float32).reshape(CTX // block_width, block_width, D_IDX)

    def index_block(key_block):
        head_dots = jnp.dot(query_flat, key_block.T)
        active = jnp.maximum(head_dots, 0.0).reshape(QROWS, H_IDX, block_width)
        return jnp.sum(active * head_weights[:, :, None], axis=1)

    blocks = lax.map(index_block, key_blocks)
    scores = jnp.moveaxis(blocks, 0, 1).reshape(QROWS, CTX)
    row_max = jnp.max(scores, axis=1, keepdims=True)
    row_total = jnp.sum(jnp.exp(scores - row_max), axis=1, keepdims=True)
    index_logp = scores - (row_max + jnp.log(row_total)) + jnp.log(CTX * 1.0)

    page_store = latent_cache.reshape(PAGES, PAGE, DK)
    logit_scale = (QK_NOPE + D_ROPE) ** -0.5

    def attend(pair):
        query_row, row_pages = pair
        key_rows = page_store[row_pages].reshape(TOPP * PAGE, DK)
        logits = jnp.dot(query_row.reshape(H, DK).astype(jnp.float32), key_rows.astype(jnp.float32).T) * logit_scale
        logit_max = jnp.max(logits, axis=1, keepdims=True)
        expo = jnp.exp(logits - logit_max)
        att_weights = (expo / jnp.sum(expo, axis=1, keepdims=True)).astype(jnp.bfloat16)
        mixed_rows = jnp.dot(att_weights, key_rows[:, :D_LAT], preferred_element_type=jnp.float32)
        return mixed_rows.astype(jnp.bfloat16).reshape(H * D_LAT)

    latent_out = lax.map(attend, (q_latent, page_ids))
    return index_logp, latent_out
```

```python
import functools

import jax
import jax.numpy as jnp
from jax import lax
from jax.experimental import pallas as pl
from jax.experimental.pallas import tpu as pltpu
from jax.sharding import PartitionSpec as P

H_IDX = 64
D_IDX = 128
H = 128
D_LAT = 512
D_ROPE = 64
QK_NOPE = 128
PAGE = 64
TOPP = 32
MOST = 2
LANES = 128
BLOB = PAGE * (D_LAT // LANES) + PAGE * D_ROPE // LANES
HALF = PAGE // 2
QROWS_MSG = 80
NEG = -1e30
MIB = 1 << 20


def pack_kernel(table_ref, cache_ref, out_ref):
    step = pl.program_id(0)
    rows = out_ref.shape[0]
    for r in range(rows):
        for s in range(MOST):
            page = jnp.maximum(table_ref[(step * rows + r) * MOST + s] - 1, 0)
            start = pl.multiple_of(page * PAGE, PAGE)
            for j in range(D_LAT // LANES):
                out_ref[r, s, j * PAGE : (j + 1) * PAGE, :] = cache_ref[
                    pl.ds(start, PAGE), j * LANES : (j + 1) * LANES
                ]
            low = cache_ref[pl.ds(start, HALF), D_LAT : D_LAT + D_ROPE]
            high = cache_ref[pl.ds(start + HALF, HALF), D_LAT : D_LAT + D_ROPE]
            out_ref[r, s, D_LAT // LANES * PAGE : BLOB, :] = jnp.concatenate([low, high], axis=1)


def pack_pages(table, cache, peers):
    rows = 4
    return pl.pallas_call(
        pack_kernel,
        grid_spec=pltpu.PrefetchScalarGridSpec(
            num_scalar_prefetch=1,
            grid=(peers // rows,),
            in_specs=[pl.BlockSpec(cache.shape, lambda i, t: (0, 0))],
            out_specs=pl.BlockSpec((rows, MOST, BLOB, LANES), lambda i, t: (i, 0, 0, 0)),
        ),
        out_shape=jax.ShapeDtypeStruct((peers, MOST, BLOB, LANES), cache.dtype),
        compiler_params=pltpu.CompilerParams(vmem_limit_bytes=24 * MIB),
        cost_estimate=pl.CostEstimate(flops=0, bytes_accessed=7 * MIB, transcendentals=0),
        name="pack_pages",
    )(table, cache)


def score_kernel(query_ref, key_ref, out_ref, weight_ref, sum_ref):
    rows = query_ref.shape[0]
    eye = lax.broadcasted_iota(jnp.int32, (H_IDX, H_IDX), 0) == lax.broadcasted_iota(
        jnp.int32, (H_IDX, H_IDX), 1
    )
    ones = jnp.ones((H_IDX, LANES), jnp.bfloat16)
    for r in range(rows):
        row = query_ref[r, H_IDX : H_IDX + 16, :][0:1, :H_IDX].astype(jnp.float32)
        diagonal = jnp.where(eye, row, 0.0).astype(jnp.bfloat16)
        weight_ref[r] = jnp.dot(diagonal, ones, preferred_element_type=jnp.float32)
    width = 2 * LANES
    for r in range(rows):
        query = query_ref[r, :H_IDX, :]
        weight = weight_ref[r]
        for b in range(key_ref.shape[0] // width):
            keys = key_ref[b * width : (b + 1) * width, :]
            dots = lax.dot_general(
                query, keys, (((1,), (1,)), ((), ())), preferred_element_type=jnp.float32
            )
            for j in range(2):
                part = jnp.maximum(dots[:, j * LANES : (j + 1) * LANES], 0.0) * weight
                sum_ref[r, 2 * b + j : 2 * b + j + 1, :] = jnp.sum(part, axis=0, keepdims=True)
        out_ref[r] = sum_ref[r].astype(out_ref.dtype)


def index_scores(queries, keys):
    rows = 4
    peers = queries.shape[0]
    blocks = keys.shape[0] // LANES
    return pl.pallas_call(
        score_kernel,
        grid=(peers // rows,),
        in_specs=[
            pl.BlockSpec((rows, QROWS_MSG, LANES), lambda i: (i, 0, 0)),
            pl.BlockSpec(keys.shape, lambda i: (0, 0)),
        ],
        out_specs=pl.BlockSpec((rows, blocks, LANES), lambda i: (i, 0, 0)),
        out_shape=jax.ShapeDtypeStruct((peers, blocks, LANES), jnp.bfloat16),
        scratch_shapes=[
            pltpu.VMEM((rows, H_IDX, LANES), jnp.float32),
            pltpu.VMEM((rows, blocks, LANES), jnp.float32),
        ],
        compiler_params=pltpu.CompilerParams(vmem_limit_bytes=16 * MIB),
        cost_estimate=pl.CostEstimate(
            flops=2 * peers * H_IDX * keys.shape[0] * D_IDX,
            bytes_accessed=2 * MIB,
            transcendentals=0,
        ),
        name="index_scores",
    )(queries, keys)


def logp_kernel(score_ref, out_ref):
    scores = score_ref[...].astype(jnp.float32)
    top = jnp.max(scores)
    total = jnp.sum(jnp.exp(scores - top), keepdims=True)
    out_ref[...] = scores - (top + jnp.log(total)) + jnp.log(jnp.float32(scores.size))


def log_distribution(scores):
    return pl.pallas_call(
        logp_kernel,
        out_shape=jax.ShapeDtypeStruct(scores.shape, jnp.float32),
        compiler_params=pltpu.CompilerParams(vmem_limit_bytes=8 * MIB),
        cost_estimate=pl.CostEstimate(
            flops=4 * scores.size, bytes_accessed=6 * scores.size, transcendentals=scores.size
        ),
        name="log_distribution",
    )(scores)


def attend_kernel(used_ref, query_ref, low_ref, high_ref, page_ref, out_ref, top_ref, total_ref, sum_ref):
    step = pl.program_id(0)
    sources = page_ref.shape[0]
    pages = sources * MOST

    @pl.when(step == 0)
    def _():
        top_ref[...] = jnp.full_like(top_ref, NEG)
        total_ref[...] = jnp.zeros_like(total_ref)
        sum_ref[...] = jnp.zeros_like(sum_ref)

    def latents(first):
        return jnp.concatenate(
            [
                jnp.concatenate(
                    [
                        page_ref[i, s, j * PAGE + first : j * PAGE + first + HALF, :]
                        for j in range(D_LAT // LANES)
                    ],
                    axis=1,
                )
                for i in range(sources)
                for s in range(MOST)
            ],
            axis=0,
        )

    rotary = jnp.concatenate(
        [
            page_ref[i, s, D_LAT // LANES * PAGE : BLOB, :]
            for i in range(sources)
            for s in range(MOST)
        ],
        axis=0,
    )
    across = (((1,), (1,)), ((), ()))
    scale = (QK_NOPE + D_ROPE) ** (-0.5)
    place = lax.broadcasted_iota(jnp.int32, (1, pages * HALF), 1) // HALF
    live = jnp.zeros((1, pages * HALF), jnp.int32)
    for p in range(pages):
        live = jnp.where(place == p, used_ref[step * pages + p], live)
    keys = [latents(0), latents(HALF)]
    logits = [
        jnp.where(
            live > 0,
            (
                lax.dot_general(query_ref[...], k, across, preferred_element_type=jnp.float32)
                + lax.dot_general(q[...], rotary, across, preferred_element_type=jnp.float32)
            )
            * scale,
            NEG,
        )
        for k, q in zip(keys, (low_ref, high_ref))
    ]
    old = top_ref[...]
    new = jnp.maximum(
        old,
        jnp.maximum(
            jnp.max(logits[0], axis=1, keepdims=True), jnp.max(logits[1], axis=1, keepdims=True)
        ),
    )
    fade = jnp.exp(old - new)
    top_ref[...] = new
    expo = [jnp.exp(v - new[:, :1]) for v in logits]
    total_ref[...] = (
        total_ref[...] * fade
        + jnp.sum(expo[0], axis=1, keepdims=True)
        + jnp.sum(expo[1], axis=1, keepdims=True)
    )
    mixed = sum(
        jnp.dot(e.astype(jnp.bfloat16), k, preferred_element_type=jnp.float32)
        for e, k in zip(expo, keys)
    )
    sum_ref[...] = sum_ref[...] * fade[:, :1] + mixed

    @pl.when(step == pl.num_programs(0) - 1)
    def _():
        out_ref[...] = (sum_ref[...] / total_ref[...][:, :1]).astype(out_ref.dtype)


def attend(used, query, pages):
    sources = 4
    peers = pages.shape[0]
    latent = query[:, :D_LAT]
    rotary = query[:, D_LAT:]
    nothing = jnp.zeros_like(rotary)
    low = jnp.concatenate([rotary, nothing], axis=1)
    high = jnp.concatenate([nothing, rotary], axis=1)
    whole = lambda shape: pl.BlockSpec(shape, lambda i, u: (0, 0))
    return pl.pallas_call(
        attend_kernel,
        grid_spec=pltpu.PrefetchScalarGridSpec(
            num_scalar_prefetch=1,
            grid=(peers // sources,),
            in_specs=[
                whole((H, D_LAT)),
                whole((H, LANES)),
                whole((H, LANES)),
                pl.BlockSpec((sources, MOST, BLOB, LANES), lambda i, u: (i, 0, 0, 0)),
            ],
            out_specs=whole((H, D_LAT)),
            scratch_shapes=[
                pltpu.VMEM((H, LANES), jnp.float32),
                pltpu.VMEM((H, LANES), jnp.float32),
                pltpu.VMEM((H, D_LAT), jnp.float32),
            ],
        ),
        out_shape=jax.ShapeDtypeStruct((H, D_LAT), jnp.bfloat16),
        compiler_params=pltpu.CompilerParams(vmem_limit_bytes=24 * MIB),
        cost_estimate=pl.CostEstimate(
            flops=2 * H * peers * MOST * PAGE * (2 * D_LAT + D_ROPE),
            bytes_accessed=5 * MIB,
            transcendentals=H * peers * MOST * PAGE,
        ),
        name="attend",
    )(used, latent, low, high, pages)


def request_table(page_ids, owners, pages_dev):
    ids = page_ids[0]
    owner, local = ids // pages_dev, ids % pages_dev
    earlier = jnp.arange(TOPP)[None, :] < jnp.arange(TOPP)[:, None]
    rank = jnp.sum(((owner[:, None] == owner[None, :]) & earlier).astype(jnp.int32), axis=1)
    chosen = (owner[None, None, :] == jnp.arange(owners)[:, None, None]) & (
        rank[None, None, :] == jnp.arange(MOST)[None, :, None]
    )
    return jnp.sum(jnp.where(chosen, local[None, None, :] + 1, 0), axis=2)


def per_device(idx_query, idx_weight, idx_keys, q_latent, latent_cache, page_ids):
    owners = lax.axis_size("ctx")
    groups = lax.axis_size("qry")
    ctx_dev = idx_keys.shape[0]
    exchange = functools.partial(lax.all_to_all, split_axis=0, concat_axis=0, tiled=True)

    table = request_table(page_ids, owners, ctx_dev // PAGE)
    wide = jnp.pad(table[:, None, :], ((0, 0), (0, 7), (0, LANES - MOST)))
    asked = exchange(wide, "ctx")[:, 0, :MOST]
    packed = pack_pages(asked.reshape(-1), latent_cache, owners)
    pages = exchange(packed, "ctx")

    heads_dev = H_IDX // groups
    parts = jnp.concatenate(
        [
            idx_query.reshape(groups, heads_dev, D_IDX),
            jnp.pad(idx_weight[:, None, :], ((0, 0), (0, 7), (0, LANES - heads_dev))),
        ],
        axis=1,
    )
    parts = exchange(parts, "qry")
    own = jnp.concatenate(
        [
            parts[:, :heads_dev, :].reshape(H_IDX, D_IDX),
            jnp.pad(
                parts[:, heads_dev, :heads_dev].reshape(1, H_IDX),
                ((0, QROWS_MSG - H_IDX - 1), (0, LANES - H_IDX)),
            ),
        ],
        axis=0,
    )
    queries = exchange(jnp.broadcast_to(own[None], (owners, QROWS_MSG, LANES)), "ctx")
    scores = exchange(index_scores(queries, idx_keys), "ctx")
    index_logp = log_distribution(scores.reshape(-1, LANES)).reshape(1, -1)

    latent_out = attend(
        table.reshape(-1), q_latent.reshape(H, D_LAT + D_ROPE), pages
    ).reshape(1, -1)
    return (index_logp, latent_out)


def solution(mesh):
    in_specs = (
        P("ctx", "qry"),
        P("ctx", "qry"),
        P("ctx", None),
        P(("ctx", "qry"), None),
        P("ctx", None),
        P(("ctx", "qry"), None),
    )
    out_specs = (P(("ctx", "qry"), None), P(("ctx", "qry"), None))
    return jax.shard_map(
        per_device, mesh=mesh, in_specs=in_specs, out_specs=out_specs, check_vma=False
    )
```

```python
import functools

import jax
import jax.numpy as jnp
from jax import lax
from jax.experimental import pallas as pl
from jax.experimental.pallas import tpu as pltpu
from jax.sharding import PartitionSpec as P

H_IDX = 64
D_IDX = 128
H = 128
D_LAT = 512
D_ROPE = 64
DK = D_LAT + D_ROPE
QK_NOPE = 128
PAGE = 64
TOPP = 32
LANES = 128
MSG = 80
NEG = -1e30
MIB = 1 << 20


def request_kernel(pages_dev, ids_ref, out_ref):
    owners = out_ref.shape[0]
    ids = ids_ref[...]
    owner, local = ids // pages_dev, ids % pages_dev
    mine = owner == lax.broadcasted_iota(jnp.int32, (owners, TOPP), 0)
    count = jnp.sum(mine.astype(jnp.int32), axis=1, keepdims=True)
    low = jnp.min(jnp.where(mine, local, pages_dev), axis=1, keepdims=True)
    high = jnp.max(jnp.where(mine, local, -1), axis=1, keepdims=True)
    first = jnp.where(count >= 1, low + 1, 0)
    second = jnp.where(count >= 2, high + 1, 0)
    lane = lax.broadcasted_iota(jnp.int32, (owners, LANES), 1)
    table = jnp.where(lane == 0, first, jnp.where(lane == 1, second, 0))
    out_ref[...] = table.reshape(owners, 1, LANES)


def request_table(page_ids, owners, pages_dev):
    return pl.pallas_call(
        functools.partial(request_kernel, pages_dev),
        out_shape=jax.ShapeDtypeStruct((owners, 1, LANES), jnp.int32),
        name="request_table",
    )(page_ids)


def tile_kernel(cache_ref, out_ref):
    for t in range(out_ref.shape[1]):
        tile = cache_ref[:, t * LANES : (t + 1) * LANES]
        out_ref[0, t] = tile
        out_ref[1, t] = jnp.concatenate([tile[:, PAGE:], tile[:, :PAGE]], axis=1)


def tile_pages(cache):
    tiles = cache.shape[1] // LANES
    step = 4
    return pl.pallas_call(
        tile_kernel,
        grid=(tiles // step,),
        in_specs=[pl.BlockSpec((DK, step * LANES), lambda i: (0, i))],
        out_specs=pl.BlockSpec((2, step, DK, LANES), lambda i: (0, i, 0, 0)),
        out_shape=jax.ShapeDtypeStruct((2, tiles, DK, LANES), cache.dtype),
        compiler_params=pltpu.CompilerParams(vmem_limit_bytes=16 * MIB),
        cost_estimate=pl.CostEstimate(flops=0, bytes_accessed=7 * MIB, transcendentals=0),
        name="tile_pages",
    )(cache)


def pack_kernel(table_ref, tile_ref, out_ref):
    step = pl.program_id(0)
    rows = out_ref.shape[0]
    left = lax.broadcasted_iota(jnp.int32, (DK, LANES), 1) < PAGE
    for r in range(rows):
        first = jnp.maximum(table_ref[step * rows + r, 0, 0] - 1, 0)
        second = jnp.maximum(table_ref[step * rows + r, 0, 1] - 1, 0)
        out_ref[r] = jnp.where(
            left, tile_ref[first % 2, first // 2], tile_ref[1 - second % 2, second // 2]
        )


def pack_pages(table, tiles):
    peers = table.shape[0]
    rows = 4
    return pl.pallas_call(
        pack_kernel,
        grid=(peers // rows,),
        in_specs=[
            pl.BlockSpec(memory_space=pltpu.SMEM),
            pl.BlockSpec(tiles.shape, lambda i: (0, 0, 0, 0)),
        ],
        out_specs=pl.BlockSpec((rows, DK, LANES), lambda i: (i, 0, 0)),
        out_shape=pltpu.HBM((peers, DK, LANES), tiles.dtype),
        compiler_params=pltpu.CompilerParams(vmem_limit_bytes=24 * MIB),
        cost_estimate=pl.CostEstimate(flops=0, bytes_accessed=9 * MIB, transcendentals=0),
        name="pack_pages",
    )(table, tiles)


def score_kernel(key_ref, *refs):
    query_refs, (out_ref, sum_ref) = refs[:-2], refs[-2:]
    eye = lax.broadcasted_iota(jnp.int32, (H_IDX, H_IDX), 0) == lax.broadcasted_iota(
        jnp.int32, (H_IDX, H_IDX), 1
    )
    ones = jnp.ones((H_IDX, LANES), jnp.bfloat16)
    width = 2 * LANES
    for g, query_ref in enumerate(query_refs):
        row = query_ref[0, H_IDX : H_IDX + 16, :][0:1, :H_IDX].astype(jnp.float32)
        diagonal = jnp.where(eye, row, 0.0).astype(jnp.bfloat16)
        weight = jnp.dot(diagonal, ones, preferred_element_type=jnp.float32)
        query = query_ref[0, :H_IDX, :]
        for b in range(key_ref.shape[0] // width):
            keys = key_ref[b * width : (b + 1) * width, :]
            dots = lax.dot_general(
                query, keys, (((1,), (1,)), ((), ())), preferred_element_type=jnp.float32
            )
            for j in range(2):
                part = jnp.maximum(dots[:, j * LANES : (j + 1) * LANES], 0.0) * weight
                sum_ref[g, 2 * b + j : 2 * b + j + 1, :] = jnp.sum(part, axis=0, keepdims=True)
        out_ref[g, 0] = sum_ref[g].astype(out_ref.dtype)


def index_scores(queries, keys):
    groups, rows = len(queries), queries[0].shape[0]
    blocks = keys.shape[0] // LANES
    return pl.pallas_call(
        score_kernel,
        grid=(rows,),
        in_specs=[pl.BlockSpec(keys.shape, lambda i: (0, 0))]
        + [pl.BlockSpec((1, MSG, LANES), lambda i: (i, 0, 0))] * groups,
        out_specs=pl.BlockSpec((groups, 1, blocks, LANES), lambda i: (0, i, 0, 0)),
        out_shape=jax.ShapeDtypeStruct((groups, rows, blocks, LANES), jnp.bfloat16),
        scratch_shapes=[pltpu.VMEM((groups, blocks, LANES), jnp.float32)],
        compiler_params=pltpu.CompilerParams(vmem_limit_bytes=16 * MIB),
        cost_estimate=pl.CostEstimate(
            flops=2 * groups * rows * H_IDX * keys.shape[0] * D_IDX,
            bytes_accessed=2 * MIB,
            transcendentals=0,
        ),
        name="index_scores",
    )(keys, *queries)


def logp_kernel(me_ref, *refs):
    part_refs, out_ref = refs[:-1], refs[-1]
    parts = [ref[...].astype(jnp.float32) for ref in part_refs]
    top = functools.reduce(jnp.maximum, [jnp.max(p) for p in parts])
    total = sum(jnp.sum(jnp.exp(p - top), axis=0) for p in parts)
    total = jnp.sum(total, keepdims=True)
    count = sum(p.size for p in parts)
    shift = jnp.log(jnp.float32(count)) - (top + jnp.log(total))
    rows = part_refs[0].shape[1]
    for g, p in enumerate(parts):
        for s in range(p.shape[0]):
            source = me_ref[0] ^ (p.shape[0] * g + s)
            out_ref[pl.ds(pl.multiple_of(source * rows, rows), rows), :] = p[s] + shift


def log_distribution(me, parts):
    count = sum(p.size for p in parts)
    return pl.pallas_call(
        logp_kernel,
        in_specs=[pl.BlockSpec(memory_space=pltpu.SMEM)]
        + [pl.BlockSpec(memory_space=pltpu.VMEM)] * len(parts),
        out_shape=jax.ShapeDtypeStruct((count // LANES, LANES), jnp.float32),
        compiler_params=pltpu.CompilerParams(vmem_limit_bytes=8 * MIB),
        cost_estimate=pl.CostEstimate(
            flops=4 * count, bytes_accessed=6 * count, transcendentals=count
        ),
        name="log_distribution",
    )(me, *parts)


def attend_kernel(used_ref, query_ref, page_ref, out_ref, top_ref, total_ref, sum_ref):
    step = pl.program_id(0)
    sources = page_ref.shape[0]

    @pl.when(step == 0)
    def _():
        top_ref[...] = jnp.full_like(top_ref, NEG)
        total_ref[...] = jnp.zeros_like(total_ref)
        sum_ref[...] = jnp.zeros_like(sum_ref)

    left = lax.broadcasted_iota(jnp.int32, (1, LANES), 1) < PAGE
    live = []
    for i in range(sources):
        slots = [
            jnp.where(used_ref[step * sources + i, 0, s] > 0, 0.0, NEG) for s in range(2)
        ]
        live.append(jnp.where(left, slots[0], slots[1]))
    live = jnp.concatenate(live, axis=1)
    keys = jnp.concatenate([page_ref[i] for i in range(sources)], axis=1)
    scale = (QK_NOPE + D_ROPE) ** (-0.5)
    logits = jnp.dot(query_ref[...], keys, preferred_element_type=jnp.float32) * scale + live
    old = top_ref[...]
    new = jnp.maximum(old, jnp.max(logits, axis=1, keepdims=True))
    fade = jnp.exp(old - new)
    top_ref[...] = new
    expo = jnp.exp(logits - new[:, :1])
    total_ref[...] = total_ref[...] * fade + jnp.sum(expo, axis=1, keepdims=True)
    mixed = lax.dot_general(
        expo.astype(jnp.bfloat16),
        keys[:D_LAT],
        (((1,), (1,)), ((), ())),
        preferred_element_type=jnp.float32,
    )
    sum_ref[...] = sum_ref[...] * fade[:, :1] + mixed

    @pl.when(step == pl.num_programs(0) - 1)
    def _():
        out_ref[...] = (sum_ref[...] / total_ref[...][:, :1]).astype(out_ref.dtype)


def attend(used, query, pages):
    sources = 8
    peers = pages.shape[0]
    tokens = peers * LANES
    return pl.pallas_call(
        attend_kernel,
        grid=(peers // sources,),
        in_specs=[
            pl.BlockSpec(memory_space=pltpu.SMEM),
            pl.BlockSpec((H, DK), lambda i: (0, 0)),
            pl.BlockSpec((sources, DK, LANES), lambda i: (i, 0, 0)),
        ],
        out_specs=pl.BlockSpec((H, D_LAT), lambda i: (0, 0)),
        scratch_shapes=[
            pltpu.VMEM((H, LANES), jnp.float32),
            pltpu.VMEM((H, LANES), jnp.float32),
            pltpu.VMEM((H, D_LAT), jnp.float32),
        ],
        out_shape=jax.ShapeDtypeStruct((H, D_LAT), jnp.bfloat16),
        compiler_params=pltpu.CompilerParams(vmem_limit_bytes=24 * MIB),
        cost_estimate=pl.CostEstimate(
            flops=2 * H * tokens * (2 * D_LAT + D_ROPE),
            bytes_accessed=5 * MIB,
            transcendentals=H * tokens,
        ),
        name="attend",
    )(used, query, pages)


def swap(x, axis, bits):
    size = lax.axis_size(axis)
    return lax.ppermute(x, axis, [(i, i ^ bits) for i in range(size)])


def head_parts(idx_query, idx_weight):
    groups = lax.axis_size("qry")
    me = lax.axis_index("qry")
    heads = idx_weight.shape[1]
    parts = jnp.concatenate(
        [
            idx_query.reshape(groups, heads, D_IDX),
            jnp.pad(idx_weight[:, None, :], ((0, 0), (0, 7), (0, LANES - heads))),
        ],
        axis=1,
    )
    got = []
    for d in range(groups):
        part = lax.dynamic_index_in_dim(parts, me ^ d, 0, False)
        got.append(swap(part, "qry", d) if d else part)
    queries = jnp.concatenate([g[:heads] for g in got], axis=0)
    weights = jnp.concatenate([g[heads, :heads] for g in got], axis=0)[None]
    return jnp.concatenate(
        [queries, jnp.pad(weights, ((0, MSG - H_IDX - 1), (0, LANES - H_IDX)))], axis=0
    )


def per_device(idx_query, idx_weight, idx_keys, q_latent, latent_cache, page_ids):
    owners = lax.axis_size("ctx")
    ctx_dev = idx_keys.shape[0]
    exchange = functools.partial(
        lax.all_to_all, axis_name="ctx", split_axis=0, concat_axis=0, tiled=True
    )

    table = request_table(page_ids, owners, ctx_dev // PAGE)
    tiles = tile_pages(latent_cache.T)
    pages = exchange(pack_pages(exchange(table), tiles))

    own = head_parts(idx_query, idx_weight)
    pair = jnp.stack([own, swap(own, "ctx", 1)])
    line = jnp.concatenate([pair] + [swap(pair, "ctx", d << 1) for d in range(1, 4)], axis=0)
    plane = [line] + [swap(line, "ctx", d << 3) for d in range(1, 4)]
    scores = index_scores(plane, idx_keys)
    scores = scores.reshape(4, 4, 2, *scores.shape[2:])
    scores = jnp.stack([scores[:, :, 0], swap(scores[:, :, 1], "ctx", 1)], axis=2)
    scores = jnp.concatenate(
        [scores[:, 0]] + [swap(scores[:, d], "ctx", d << 1) for d in range(1, 4)], axis=1
    )
    scores = [scores[0]] + [swap(scores[d], "ctx", d << 3) for d in range(1, 4)]
    me = lax.axis_index("ctx").astype(jnp.int32).reshape(1)
    index_logp = log_distribution(me, scores).reshape(1, -1)

    latent_out = attend(table, q_latent.reshape(H, DK), pages).reshape(1, -1)
    return (index_logp, latent_out)


def solution(mesh):
    in_specs = (
        P("ctx", "qry"),
        P("ctx", "qry"),
        P("ctx", None),
        P(("ctx", "qry"), None),
        P("ctx", None),
        P(("ctx", "qry"), None),
    )
    out_specs = (P(("ctx", "qry"), None), P(("ctx", "qry"), None))
    return jax.shard_map(
        per_device, mesh=mesh, in_specs=in_specs, out_specs=out_specs, check_vma=False
    )
```

```python
import functools

import jax
import jax.numpy as jnp
from jax import lax
from jax.experimental import pallas as pl
from jax.experimental.pallas import tpu as pltpu
from jax.sharding import PartitionSpec as P

H_IDX = 64
D_IDX = 128
H = 128
D_LAT = 512
D_ROPE = 64
DK = D_LAT + D_ROPE
QK_NOPE = 128
PAGE = 64
TOPP = 32
LANES = 128
NEG = -1e30
MIB = 1 << 20


def request_kernel(pages_dev, ids_ref, query_ref, weight_ref, out_ref, table_ref):
    owners = out_ref.shape[0]
    rows, heads = weight_ref.shape
    ids = ids_ref[...]
    owner, local = ids // pages_dev, ids % pages_dev
    mine = owner == lax.broadcasted_iota(jnp.int32, (owners, TOPP), 0)
    low = jnp.min(jnp.where(mine, local, pages_dev), axis=1, keepdims=True)
    high = jnp.max(jnp.where(mine, local, -1), axis=1, keepdims=True)
    turn = (low < high) & (low % 2 == 1) & (high % 2 == 0)
    first = jnp.where(turn, high, low)
    second = jnp.where(turn, low, high)
    single = low == high
    left = jnp.where((high < 0) | (single & (low % 2 == 1)), 0, first + 1)
    right = jnp.where((high < 0) | (single & (low % 2 == 0)), 0, second + 1)
    lane = lax.broadcasted_iota(jnp.int32, (owners, LANES), 1)
    table = jnp.where(lane == 0, left, jnp.where(lane == 1, right, 0)).reshape(owners, 1, LANES)
    table_ref[...] = table
    weight = jnp.concatenate(
        [weight_ref[...].astype(jnp.float32), jnp.zeros((rows, LANES - heads), jnp.float32)], axis=1
    )
    asked = jnp.broadcast_to(table.astype(jnp.float32), (owners, rows, LANES))
    tail = jnp.concatenate(
        [jnp.broadcast_to(weight[None], (owners, rows, LANES)), asked], axis=1
    )
    out_ref[:, : rows * heads, :] = jnp.broadcast_to(
        query_ref[...][None], (owners, rows * heads, LANES)
    )
    out_ref[:, rows * heads :, :] = tail.astype(out_ref.dtype)


def requests(page_ids, query, weight, owners, pages_dev):
    length = query.shape[0] + 2 * weight.shape[0]
    return pl.pallas_call(
        functools.partial(request_kernel, pages_dev),
        out_shape=(
            pltpu.HBM((owners, length, LANES), query.dtype),
            jax.ShapeDtypeStruct((owners, 1, LANES), jnp.int32),
        ),
        name="requests",
    )(page_ids, query, weight)


def pack_kernel(table_ref, cache_ref, out_ref):
    step = pl.program_id(0)
    rows = out_ref.shape[0]
    left = lax.broadcasted_iota(jnp.int32, (DK, LANES), 1) < PAGE

    def tile(page):
        return cache_ref[:, pl.ds(pl.multiple_of(page // 2 * LANES, LANES), LANES)]

    def turned(x):
        return jnp.concatenate([x[:, PAGE:], x[:, :PAGE]], axis=1)

    for r in range(rows):
        first = table_ref[step * rows + r, 0]
        second = table_ref[step * rows + r, 1]
        first = jnp.where(first > 0, first - 1, 0)
        second = jnp.where(second > 0, second - 1, 1)
        straight = (first % 2 == 0) & (second % 2 == 1)

        @pl.when(straight)
        def _(r=r, first=first, second=second):
            out_ref[r] = jnp.where(left, tile(first), tile(second))

        @pl.when(jnp.logical_not(straight))
        def _(r=r, first=first, second=second):
            a, b = tile(first), tile(second)
            a = jnp.where(first % 2 == 0, a, turned(a))
            b = jnp.where(second % 2 == 1, b, turned(b))
            out_ref[r] = jnp.where(left, a, b)


def pack_pages(table, cache):
    peers = table.shape[0]
    rows = 4
    return pl.pallas_call(
        pack_kernel,
        grid=(peers // rows,),
        in_specs=[
            pl.BlockSpec(memory_space=pltpu.SMEM),
            pl.BlockSpec(cache.shape, lambda i: (0, 0)),
        ],
        out_specs=pl.BlockSpec((rows, DK, LANES), lambda i: (i, 0, 0)),
        out_shape=pltpu.HBM((peers, DK, LANES), cache.dtype),
        compiler_params=pltpu.CompilerParams(vmem_limit_bytes=24 * MIB),
        cost_estimate=pl.CostEstimate(flops=0, bytes_accessed=7 * MIB, transcendentals=0),
        name="pack_pages",
    )(table, cache)


def score_kernel(query_ref, key_ref, out_ref, sum_ref):
    sources = query_ref.shape[0]
    rows = out_ref.shape[0]
    heads = (query_ref.shape[1] - 2 * rows) // rows
    flat = rows * heads
    blocks = key_ref.shape[0] // LANES
    queries = jnp.concatenate([query_ref[i, :flat, :] for i in range(sources)], axis=0)
    weights = []
    for i in range(sources):
        tail = query_ref[i, flat:, :].astype(jnp.float32)[:rows]
        weights.append(
            [jnp.broadcast_to(tail[:, h : h + 1], (rows, LANES)) for h in range(heads)]
        )
    for b in range(blocks // 2):
        keys = key_ref[2 * b * LANES : 2 * (b + 1) * LANES, :]
        dots = lax.dot_general(
            queries, keys, (((1,), (1,)), ((), ())), preferred_element_type=jnp.float32
        )
        for j in range(2):
            for i in range(sources):
                total = None
                for h in range(heads):
                    at = i * flat + h * rows
                    part = (
                        jnp.maximum(dots[at : at + rows, j * LANES : (j + 1) * LANES], 0.0)
                        * weights[i][h]
                    )
                    total = part if total is None else total + part
                sum_ref[i, pl.ds(2 * b + j, rows, stride=blocks), :] = total
    for i in range(sources):
        for r in range(rows):
            out_ref[r, i] = sum_ref[i, r * blocks : (r + 1) * blocks, :]


def index_scores(queries, keys, rows):
    sources = 4
    peers, length = queries.shape[:2]
    blocks = keys.shape[0] // LANES
    return pl.pallas_call(
        score_kernel,
        grid=(peers // sources,),
        in_specs=[
            pl.BlockSpec((sources, length, LANES), lambda i: (i, 0, 0)),
            pl.BlockSpec(keys.shape, lambda i: (0, 0)),
        ],
        out_specs=pl.BlockSpec((rows, sources, blocks, LANES), lambda i: (0, i, 0, 0)),
        out_shape=jax.ShapeDtypeStruct((rows, peers, blocks, LANES), jnp.float32),
        scratch_shapes=[pltpu.VMEM((sources, rows * blocks, LANES), jnp.float32)],
        compiler_params=pltpu.CompilerParams(vmem_limit_bytes=16 * MIB),
        cost_estimate=pl.CostEstimate(
            flops=2 * peers * length * keys.shape[0] * D_IDX,
            bytes_accessed=2 * MIB,
            transcendentals=0,
        ),
        name="index_scores",
    )(queries, keys)


def logp_kernel(score_ref, out_ref):
    scores = score_ref[...].astype(jnp.float32)
    top = jnp.max(scores)
    total = jnp.sum(jnp.exp(scores - top), keepdims=True)
    out_ref[...] = scores - (top + jnp.log(total)) + jnp.log(jnp.float32(scores.size))


def log_distribution(scores):
    return pl.pallas_call(
        logp_kernel,
        out_shape=jax.ShapeDtypeStruct(scores.shape, jnp.float32),
        compiler_params=pltpu.CompilerParams(vmem_limit_bytes=8 * MIB),
        cost_estimate=pl.CostEstimate(
            flops=4 * scores.size, bytes_accessed=6 * scores.size, transcendentals=scores.size
        ),
        name="log_distribution",
    )(scores)


def attend_kernel(used_ref, query_ref, page_ref, out_ref, top_ref, total_ref, sum_ref):
    step = pl.program_id(0)
    sources = page_ref.shape[0]

    @pl.when(step == 0)
    def _():
        top_ref[...] = jnp.full_like(top_ref, NEG)
        total_ref[...] = jnp.zeros_like(total_ref)
        sum_ref[...] = jnp.zeros_like(sum_ref)

    left = lax.broadcasted_iota(jnp.int32, (1, LANES), 1) < PAGE
    live = []
    for i in range(sources):
        slots = [
            jnp.where(used_ref[step * sources + i, 0, s] > 0, 0.0, NEG) for s in range(2)
        ]
        live.append(jnp.where(left, slots[0], slots[1]))
    live = jnp.concatenate(live, axis=1)
    keys = jnp.concatenate([page_ref[i] for i in range(sources)], axis=1)
    scale = (QK_NOPE + D_ROPE) ** (-0.5)
    logits = jnp.dot(query_ref[...], keys, preferred_element_type=jnp.float32) * scale + live
    old = top_ref[...]
    new = jnp.maximum(old, jnp.max(logits, axis=1, keepdims=True))
    fade = jnp.exp(old - new)
    top_ref[...] = new
    expo = jnp.exp(logits - new[:, :1])
    total_ref[...] = total_ref[...] * fade + jnp.sum(expo, axis=1, keepdims=True)
    mixed = lax.dot_general(
        expo.astype(jnp.bfloat16),
        keys[:D_LAT],
        (((1,), (1,)), ((), ())),
        preferred_element_type=jnp.float32,
    )
    sum_ref[...] = sum_ref[...] * fade[:, :1] + mixed

    @pl.when(step == pl.num_programs(0) - 1)
    def _():
        out_ref[...] = (sum_ref[...] / total_ref[...][:, :1]).astype(out_ref.dtype)


def attend(used, query, pages):
    sources = 8
    peers = pages.shape[0]
    tokens = peers * LANES
    return pl.pallas_call(
        attend_kernel,
        grid=(peers // sources,),
        in_specs=[
            pl.BlockSpec(memory_space=pltpu.SMEM),
            pl.BlockSpec((H, DK), lambda i: (0, 0)),
            pl.BlockSpec((sources, DK, LANES), lambda i: (i, 0, 0)),
        ],
        out_specs=pl.BlockSpec((H, D_LAT), lambda i: (0, 0)),
        scratch_shapes=[
            pltpu.VMEM((H, LANES), jnp.float32),
            pltpu.VMEM((H, LANES), jnp.float32),
            pltpu.VMEM((H, D_LAT), jnp.float32),
        ],
        out_shape=jax.ShapeDtypeStruct((H, D_LAT), jnp.bfloat16),
        compiler_params=pltpu.CompilerParams(vmem_limit_bytes=24 * MIB),
        cost_estimate=pl.CostEstimate(
            flops=2 * H * tokens * (2 * D_LAT + D_ROPE),
            bytes_accessed=5 * MIB,
            transcendentals=H * tokens,
        ),
        name="attend",
    )(used, query, pages)


def per_device(idx_query, idx_weight, idx_keys, q_latent, latent_cache, page_ids):
    owners = lax.axis_size("ctx")
    rows, heads = idx_weight.shape
    exchange = functools.partial(
        lax.all_to_all, axis_name="ctx", split_axis=0, concat_axis=0, tiled=True
    )

    query = idx_query.reshape(rows, heads, D_IDX).transpose(1, 0, 2).reshape(-1, D_IDX)
    sent, table = requests(page_ids, query, idx_weight, owners, idx_keys.shape[0] // PAGE)
    got = exchange(sent)
    asked = got[:, rows * heads + rows, :2].astype(jnp.int32)
    pages = exchange(pack_pages(asked, latent_cache.T))

    scores = index_scores(got, idx_keys, rows)
    scores = lax.psum_scatter(scores, "qry", scatter_dimension=0)
    scores, pages = lax.optimization_barrier((scores, pages))
    scores = exchange(scores.astype(jnp.bfloat16))
    index_logp = log_distribution(scores.reshape(-1, LANES)).reshape(1, -1)

    latent_out = attend(table, q_latent.reshape(H, DK), pages).reshape(1, -1)
    return (index_logp, latent_out)


def solution(mesh):
    in_specs = (
        P("ctx", "qry"),
        P("ctx", "qry"),
        P("ctx", None),
        P(("ctx", "qry"), None),
        P("ctx", None),
        P(("ctx", "qry"), None),
    )
    out_specs = (P(("ctx", "qry"), None), P(("ctx", "qry"), None))
    return jax.shard_map(
        per_device, mesh=mesh, in_specs=in_specs, out_specs=out_specs, check_vma=False
    )
```

```python
import functools

import jax
import jax.numpy as jnp
from jax import lax
from jax.experimental import pallas as pl
from jax.experimental.pallas import tpu as pltpu
from jax.sharding import PartitionSpec as P

H_IDX = 64
D_IDX = 128
H = 128
D_LAT = 512
D_ROPE = 64
DK = D_LAT + D_ROPE
QK_NOPE = 128
PAGE = 64
TOPP = 32
LANES = 128
NEG = -1e30
MIB = 1 << 20


def request_kernel(pages_dev, ids_ref, query_ref, weight_ref, out_ref, table_ref):
    owners = out_ref.shape[0]
    rows, heads = weight_ref.shape
    ids = ids_ref[...]
    owner, local = ids // pages_dev, ids % pages_dev
    mine = owner == lax.broadcasted_iota(jnp.int32, (owners, TOPP), 0)
    low = jnp.min(jnp.where(mine, local, pages_dev), axis=1, keepdims=True)
    high = jnp.max(jnp.where(mine, local, -1), axis=1, keepdims=True)
    turn = (low < high) & (low % 2 == 1) & (high % 2 == 0)
    first = jnp.where(turn, high, low)
    second = jnp.where(turn, low, high)
    single = low == high
    left = jnp.where((high < 0) | (single & (low % 2 == 1)), 0, first + 1)
    right = jnp.where((high < 0) | (single & (low % 2 == 0)), 0, second + 1)
    lane = lax.broadcasted_iota(jnp.int32, (owners, LANES), 1)
    table = jnp.where(lane == 0, left, jnp.where(lane == 1, right, 0)).reshape(owners, 1, LANES)
    table_ref[...] = table
    weight = jnp.concatenate(
        [weight_ref[...].astype(jnp.float32), jnp.zeros((rows, LANES - heads), jnp.float32)], axis=1
    )
    asked = jnp.broadcast_to(table.astype(jnp.float32), (owners, rows, LANES))
    out_ref[:, :rows] = jnp.broadcast_to(
        query_ref[...].reshape(1, rows, heads, LANES), (owners, rows, heads, LANES)
    )
    out_ref[:, rows] = jnp.broadcast_to(weight[None], (owners, rows, LANES)).astype(out_ref.dtype)
    out_ref[:, rows + 1] = asked.astype(out_ref.dtype)


def requests(page_ids, query, weight, owners, pages_dev):
    rows, heads = weight.shape
    return pl.pallas_call(
        functools.partial(request_kernel, pages_dev),
        out_shape=(
            pltpu.HBM((owners, rows + 2, heads, LANES), query.dtype),
            jax.ShapeDtypeStruct((owners, 1, LANES), jnp.int32),
        ),
        name="requests",
    )(page_ids, query, weight)


PIECES = 8


def pack_kernel(table_ref, cache_hbm, out_ref, cache_ref, sems):
    step = pl.program_id(0)
    rows = out_ref.shape[0]
    left = lax.broadcasted_iota(jnp.int32, (DK, LANES), 1) < PAGE

    @pl.when(step == 0)
    def _():
        width = cache_ref.shape[1] // PIECES
        copies = [
            pltpu.make_async_copy(
                cache_hbm.at[:, pl.ds(i * width, width)],
                cache_ref.at[:, pl.ds(i * width, width)],
                sems.at[i],
            )
            for i in range(PIECES)
        ]
        for copy in copies:
            copy.start()
        for copy in copies:
            copy.wait()

    def tile(page):
        return cache_ref[:, pl.ds(pl.multiple_of(page // 2 * LANES, LANES), LANES)]

    def turned(x):
        return jnp.concatenate([x[:, PAGE:], x[:, :PAGE]], axis=1)

    for r in range(rows):
        first = table_ref[step * rows + r, 0]
        second = table_ref[step * rows + r, 1]
        first = jnp.where(first > 0, first - 1, 0)
        second = jnp.where(second > 0, second - 1, 1)
        straight = (first % 2 == 0) & (second % 2 == 1)

        @pl.when(straight)
        def _(r=r, first=first, second=second):
            out_ref[r] = jnp.where(left, tile(first), tile(second))

        @pl.when(jnp.logical_not(straight))
        def _(r=r, first=first, second=second):
            a, b = tile(first), tile(second)
            a = jnp.where(first % 2 == 0, a, turned(a))
            b = jnp.where(second % 2 == 1, b, turned(b))
            out_ref[r] = jnp.where(left, a, b)


def pack_pages(table, cache):
    peers = table.shape[0]
    rows = 4
    return pl.pallas_call(
        pack_kernel,
        grid=(peers // rows,),
        in_specs=[
            pl.BlockSpec(memory_space=pltpu.SMEM),
            pl.BlockSpec(memory_space=pltpu.HBM),
        ],
        out_specs=pl.BlockSpec((rows, DK, LANES), lambda i: (i, 0, 0)),
        out_shape=pltpu.HBM((peers, DK, LANES), cache.dtype),
        scratch_shapes=[
            pltpu.VMEM(cache.shape, cache.dtype),
            pltpu.SemaphoreType.DMA((PIECES,)),
        ],
        compiler_params=pltpu.CompilerParams(vmem_limit_bytes=60 * MIB),
        cost_estimate=pl.CostEstimate(flops=0, bytes_accessed=7 * MIB, transcendentals=0),
        name="pack_pages",
    )(table, cache)


def partner_kernel(me_ref, got_ref, *out_refs):
    peers = got_ref.shape[0]
    rows = len(out_refs)
    weights = got_ref[:, rows].astype(jnp.float32)
    place = lax.broadcasted_iota(jnp.int32, weights.shape, 1)
    for d, out_ref in enumerate(out_refs):
        row = me_ref[0] ^ d
        out_ref[:peers] = got_ref[:, row]
        weight = jnp.sum(jnp.where(place == row, weights, 0.0), axis=1)
        out_ref[peers:] = weight.reshape(peers // 8, 8, LANES).astype(out_ref.dtype)


def partner_parts(me, got, rows):
    peers, _, heads, _ = got.shape
    part = jax.ShapeDtypeStruct((peers + peers // 8, heads, LANES), got.dtype)
    return pl.pallas_call(
        partner_kernel,
        in_specs=[
            pl.BlockSpec(memory_space=pltpu.SMEM),
            pl.BlockSpec(memory_space=pltpu.VMEM),
        ],
        out_shape=(part,) * rows,
        compiler_params=pltpu.CompilerParams(vmem_limit_bytes=16 * MIB),
        cost_estimate=pl.CostEstimate(flops=0, bytes_accessed=2 * MIB, transcendentals=0),
        name="partner_parts",
    )(me, got)


def score_kernel(key_ref, *refs):
    part_refs, (out_ref, sum_ref) = refs[:-2], refs[-2:]
    step = pl.program_id(0)
    sources = out_ref.shape[0]
    peers = part_refs[0].shape[0] // 9 * 8
    blocks = key_ref.shape[0] // LANES
    heads = part_refs[0].shape[1]
    flat = heads * len(part_refs)
    queries = jnp.concatenate(
        [ref[step * sources + i] for i in range(sources) for ref in part_refs], axis=0
    )
    corner = lax.broadcasted_iota(jnp.int32, (heads, LANES), 0) == lax.broadcasted_iota(
        jnp.int32, (heads, LANES), 1
    )
    tails = [ref[peers + step // 2].astype(jnp.float32) for ref in part_refs]
    half = step % 2 == 0
    weights = []
    for i in range(sources):
        for tail in tails:
            row = jnp.where(half, tail[i : i + 1], tail[sources + i : sources + i + 1])
            column = jnp.sum(jnp.where(corner, row, 0.0), axis=1, keepdims=True)
            weights.append(jnp.broadcast_to(column, (heads, LANES)))
    for b in range(blocks // 2):
        keys = key_ref[2 * b * LANES : 2 * (b + 1) * LANES, :]
        dots = lax.dot_general(
            queries, keys, (((1,), (1,)), ((), ())), preferred_element_type=jnp.float32
        )
        for j in range(2):
            for i in range(sources):
                total = None
                for d in range(len(part_refs)):
                    at = i * flat + d * heads
                    part = (
                        jnp.maximum(dots[at : at + heads, j * LANES : (j + 1) * LANES], 0.0)
                        * weights[i * len(part_refs) + d]
                    )
                    total = part if total is None else total + part
                sum_ref[i, 2 * b + j : 2 * b + j + 1, :] = jnp.sum(total, axis=0, keepdims=True)
    for i in range(sources):
        out_ref[i] = sum_ref[i].astype(out_ref.dtype)


def index_scores(keys, parts):
    sources = 4
    peers = parts[0].shape[0] // 9 * 8
    blocks = keys.shape[0] // LANES
    return pl.pallas_call(
        score_kernel,
        grid=(peers // sources,),
        in_specs=[pl.BlockSpec(memory_space=pltpu.VMEM)] * (1 + len(parts)),
        out_specs=pl.BlockSpec((sources, blocks, LANES), lambda i: (i, 0, 0)),
        out_shape=jax.ShapeDtypeStruct((peers, blocks, LANES), jnp.bfloat16),
        scratch_shapes=[pltpu.VMEM((sources, blocks, LANES), jnp.float32)],
        compiler_params=pltpu.CompilerParams(vmem_limit_bytes=16 * MIB),
        cost_estimate=pl.CostEstimate(
            flops=2 * peers * H_IDX * keys.shape[0] * D_IDX,
            bytes_accessed=2 * MIB,
            transcendentals=0,
        ),
        name="index_scores",
    )(keys, *parts)


def logp_kernel(score_ref, out_ref):
    scores = score_ref[...].astype(jnp.float32)
    top = jnp.max(scores)
    total = jnp.sum(jnp.exp(scores - top), keepdims=True)
    out_ref[...] = scores - (top + jnp.log(total)) + jnp.log(jnp.float32(scores.size))


def log_distribution(scores):
    return pl.pallas_call(
        logp_kernel,
        out_shape=jax.ShapeDtypeStruct(scores.shape, jnp.float32),
        compiler_params=pltpu.CompilerParams(vmem_limit_bytes=8 * MIB),
        cost_estimate=pl.CostEstimate(
            flops=4 * scores.size, bytes_accessed=6 * scores.size, transcendentals=scores.size
        ),
        name="log_distribution",
    )(scores)


def attend_kernel(used_ref, query_ref, page_ref, out_ref, top_ref, total_ref, sum_ref):
    step = pl.program_id(0)
    sources = page_ref.shape[0]

    @pl.when(step == 0)
    def _():
        top_ref[...] = jnp.full_like(top_ref, NEG)
        total_ref[...] = jnp.zeros_like(total_ref)
        sum_ref[...] = jnp.zeros_like(sum_ref)

    left = lax.broadcasted_iota(jnp.int32, (1, LANES), 1) < PAGE
    live = []
    for i in range(sources):
        slots = [
            jnp.where(used_ref[step * sources + i, 0, s] > 0, 0.0, NEG) for s in range(2)
        ]
        live.append(jnp.where(left, slots[0], slots[1]))
    live = jnp.concatenate(live, axis=1)
    keys = jnp.concatenate([page_ref[i] for i in range(sources)], axis=1)
    scale = (QK_NOPE + D_ROPE) ** (-0.5)
    logits = jnp.dot(query_ref[...], keys, preferred_element_type=jnp.float32) * scale + live
    old = top_ref[...]
    new = jnp.maximum(old, jnp.max(logits, axis=1, keepdims=True))
    fade = jnp.exp(old - new)
    top_ref[...] = new
    expo = jnp.exp(logits - new[:, :1])
    total_ref[...] = total_ref[...] * fade + jnp.sum(expo, axis=1, keepdims=True)
    mixed = lax.dot_general(
        expo.astype(jnp.bfloat16),
        keys[:D_LAT],
        (((1,), (1,)), ((), ())),
        preferred_element_type=jnp.float32,
    )
    sum_ref[...] = sum_ref[...] * fade[:, :1] + mixed

    @pl.when(step == pl.num_programs(0) - 1)
    def _():
        out_ref[...] = (sum_ref[...] / total_ref[...][:, :1]).astype(out_ref.dtype)


def attend(used, query, pages):
    sources = 8
    peers = pages.shape[0]
    tokens = peers * LANES
    return pl.pallas_call(
        attend_kernel,
        grid=(peers // sources,),
        in_specs=[
            pl.BlockSpec(memory_space=pltpu.SMEM),
            pl.BlockSpec((H, DK), lambda i: (0, 0)),
            pl.BlockSpec((sources, DK, LANES), lambda i: (i, 0, 0)),
        ],
        out_specs=pl.BlockSpec((H, D_LAT), lambda i: (0, 0)),
        scratch_shapes=[
            pltpu.VMEM((H, LANES), jnp.float32),
            pltpu.VMEM((H, LANES), jnp.float32),
            pltpu.VMEM((H, D_LAT), jnp.float32),
        ],
        out_shape=jax.ShapeDtypeStruct((H, D_LAT), jnp.bfloat16),
        compiler_params=pltpu.CompilerParams(vmem_limit_bytes=24 * MIB),
        cost_estimate=pl.CostEstimate(
            flops=2 * H * tokens * (2 * D_LAT + D_ROPE),
            bytes_accessed=5 * MIB,
            transcendentals=H * tokens,
        ),
        name="attend",
    )(used, query, pages)


def per_device(idx_query, idx_weight, idx_keys, q_latent, latent_cache, page_ids):
    owners = lax.axis_size("ctx")
    groups = lax.axis_size("qry")
    rows, heads = idx_weight.shape
    exchange = functools.partial(
        lax.all_to_all, axis_name="ctx", split_axis=0, concat_axis=0, tiled=True
    )

    query = idx_query.reshape(rows, heads, D_IDX)
    sent, table = requests(page_ids, query, idx_weight, owners, idx_keys.shape[0] // PAGE)
    got = exchange(sent)
    asked = got[:, rows + 1, 0, :2].astype(jnp.int32)
    pages = exchange(pack_pages(asked, latent_cache.T))

    me = lax.axis_index("qry").astype(jnp.int32).reshape(1)
    parts = partner_parts(me, got, rows)
    parts = [parts[0]] + [
        lax.ppermute(parts[d], "qry", [(i, i ^ d) for i in range(groups)])
        for d in range(1, groups)
    ]
    scores = index_scores(idx_keys, parts)
    latent = q_latent.reshape(H, DK)
    scores, pages, latent = lax.optimization_barrier((scores, pages, latent))
    scores = exchange(scores)
    index_logp = log_distribution(scores.reshape(-1, LANES)).reshape(1, -1)

    latent_out = attend(table, latent, pages).reshape(1, -1)
    return (index_logp, latent_out)


def solution(mesh):
    in_specs = (
        P("ctx", "qry"),
        P("ctx", "qry"),
        P("ctx", None),
        P(("ctx", "qry"), None),
        P("ctx", None),
        P(("ctx", "qry"), None),
    )
    out_specs = (P(("ctx", "qry"), None), P(("ctx", "qry"), None))
    return jax.shard_map(
        per_device, mesh=mesh, in_specs=in_specs, out_specs=out_specs, check_vma=False
    )
```

```python
import functools

import jax
import jax.numpy as jnp
from jax import lax
from jax.experimental import pallas as pl
from jax.experimental.pallas import tpu as pltpu
from jax.sharding import PartitionSpec as P

H_IDX = 64
D_IDX = 128
H = 128
D_LAT = 512
D_ROPE = 64
DK = D_LAT + D_ROPE
QK_NOPE = 128
PAGE = 64
TOPP = 32
LANES = 128
NEG = -1e30
FIRST = 320
MIB = 1 << 20


def request_kernel(pages_dev, ids_ref, query_ref, weight_ref, out_ref, table_ref, turn_ref):
    owners = out_ref.shape[0]
    rows, heads = weight_ref.shape
    part = rows // 2
    ids = ids_ref[...]
    owner, local = ids // pages_dev, ids % pages_dev
    mine = owner == lax.broadcasted_iota(jnp.int32, (owners, TOPP), 0)
    low = jnp.min(jnp.where(mine, local, pages_dev), axis=1, keepdims=True)
    high = jnp.max(jnp.where(mine, local, -1), axis=1, keepdims=True)
    turn = (low < high) & (low % 2 == 1) & (high % 2 == 0)
    first = jnp.where(turn, high, low)
    second = jnp.where(turn, low, high)
    single = low == high
    left = jnp.where((high < 0) | (single & (low % 2 == 1)), 0, first + 1)
    right = jnp.where((high < 0) | (single & (low % 2 == 0)), 0, second + 1)
    lane = lax.broadcasted_iota(jnp.int32, (owners, LANES), 1)
    table = jnp.where(lane == 0, left, jnp.where(lane == 1, right, 0)).reshape(owners, 1, LANES)
    table_ref[...] = table
    weight = jnp.concatenate(
        [weight_ref[...].astype(jnp.float32), jnp.zeros((rows, LANES - heads), jnp.float32)], axis=1
    )
    asked = jnp.broadcast_to(table.astype(jnp.float32), (owners, rows, LANES))
    for h in range(heads):
        turn_ref[pl.ds(h, rows, stride=heads), :] = query_ref[
            :, h * LANES : (h + 1) * LANES
        ].astype(jnp.float32)
    query = turn_ref[...].astype(out_ref.dtype).reshape(rows, heads, LANES)
    for t in range(owners):
        out_ref[t, :part] = query[t % 2 * part : (t % 2 + 1) * part]
    out_ref[:, part] = jnp.broadcast_to(weight[None], (owners, rows, LANES)).astype(out_ref.dtype)
    out_ref[:, part + 1] = asked.astype(out_ref.dtype)


def requests(page_ids, query, weight, owners, pages_dev):
    rows, heads = weight.shape
    return pl.pallas_call(
        functools.partial(request_kernel, pages_dev),
        out_shape=(
            pltpu.HBM((owners, rows // 2 + 2, heads, LANES), query.dtype),
            jax.ShapeDtypeStruct((owners, 1, LANES), jnp.int32),
        ),
        scratch_shapes=[pltpu.VMEM((rows * heads, LANES), jnp.float32)],
        name="requests",
    )(page_ids, query, weight)


GROUP = 4


def pack_kernel(first_row, table_ref, cache_hbm, *refs):
    score_refs, (out_hbm, cache_ref, stage_ref, in_sem, out_sems) = refs[:-5], refs[-5:]
    peers = stage_ref.shape[0]
    depth = cache_ref.shape[0]
    load = pltpu.make_async_copy(cache_hbm.at[pl.ds(first_row, depth)], cache_ref, in_sem)
    load.start()
    for score_ref in score_refs:
        stage_ref[:, depth:, :] = score_ref[...]
    left = lax.broadcasted_iota(jnp.int32, (depth, LANES), 1) < PAGE
    load.wait()

    def tile(page):
        return cache_ref[:, pl.ds(pl.multiple_of(page // 2 * LANES, LANES), LANES)]

    def turned(x):
        return jnp.concatenate([x[:, PAGE:], x[:, :PAGE]], axis=1)

    def send(g):
        rows = pl.ds(g * GROUP, GROUP)
        return pltpu.make_async_copy(stage_ref.at[rows], out_hbm.at[rows], out_sems.at[g])

    for r in range(peers):
        first = table_ref[r, 0]
        second = table_ref[r, 1]
        first = jnp.where(first > 0, first - 1, 0)
        second = jnp.where(second > 0, second - 1, 1)
        straight = (first % 2 == 0) & (second % 2 == 1)

        @pl.when(straight)
        def _(r=r, first=first, second=second):
            stage_ref[r, :depth] = jnp.where(left, tile(first), tile(second))

        @pl.when(jnp.logical_not(straight))
        def _(r=r, first=first, second=second):
            a, b = tile(first), tile(second)
            a = jnp.where(first % 2 == 0, a, turned(a))
            b = jnp.where(second % 2 == 1, b, turned(b))
            stage_ref[r, :depth] = jnp.where(left, a, b)

        if r % GROUP == GROUP - 1:
            send(r // GROUP).start()
    for g in range(peers // GROUP):
        send(g).wait()


def pack_pages(table, cache, first_row, depth, *scores):
    peers = table.shape[0]
    length = depth + sum(s.shape[1] for s in scores)
    return pl.pallas_call(
        functools.partial(pack_kernel, first_row),
        in_specs=[
            pl.BlockSpec(memory_space=pltpu.SMEM),
            pl.BlockSpec(memory_space=pltpu.HBM),
        ]
        + [pl.BlockSpec(memory_space=pltpu.VMEM)] * len(scores),
        out_specs=pl.BlockSpec(memory_space=pltpu.HBM),
        out_shape=pltpu.HBM((peers, length, LANES), cache.dtype),
        scratch_shapes=[
            pltpu.VMEM((depth, cache.shape[1]), cache.dtype),
            pltpu.VMEM((peers, length, LANES), cache.dtype),
            pltpu.SemaphoreType.DMA,
            pltpu.SemaphoreType.DMA((peers // GROUP,)),
        ],
        compiler_params=pltpu.CompilerParams(vmem_limit_bytes=60 * MIB),
        cost_estimate=pl.CostEstimate(flops=0, bytes_accessed=8 * MIB, transcendentals=0),
        name="pack_pages",
    )(table, cache, *scores)


def partner_kernel(place_ref, got_ref, other_ref, *out_refs):
    peers, part = got_ref.shape[0], got_ref.shape[1] - 2
    weights = got_ref[:, part].astype(jnp.float32)
    place = lax.broadcasted_iota(jnp.int32, weights.shape, 1)
    for d, out_ref in enumerate(out_refs):
        row = place_ref[0] ^ d
        mine = row // part == place_ref[1]

        @pl.when(mine)
        def _(out_ref=out_ref, row=row):
            out_ref[:peers] = got_ref[:, row % part]

        @pl.when(jnp.logical_not(mine))
        def _(out_ref=out_ref, row=row):
            out_ref[:peers] = other_ref[:, row % part]

        weight = jnp.sum(jnp.where(place == row, weights, 0.0), axis=1)
        out_ref[peers:] = weight.reshape(peers // 8, 8, LANES).astype(out_ref.dtype)


def partner_parts(place, got, other, rows):
    peers, _, heads, _ = got.shape
    part = jax.ShapeDtypeStruct((peers + peers // 8, heads, LANES), got.dtype)
    return pl.pallas_call(
        partner_kernel,
        in_specs=[
            pl.BlockSpec(memory_space=pltpu.SMEM),
            pl.BlockSpec(memory_space=pltpu.VMEM),
            pl.BlockSpec(memory_space=pltpu.VMEM),
        ],
        out_shape=(part,) * rows,
        compiler_params=pltpu.CompilerParams(vmem_limit_bytes=16 * MIB),
        cost_estimate=pl.CostEstimate(flops=0, bytes_accessed=2 * MIB, transcendentals=0),
        name="partner_parts",
    )(place, got, other)


def score_kernel(key_ref, *refs):
    part_refs, (out_ref, sum_ref) = refs[:-2], refs[-2:]
    step = pl.program_id(0)
    sources = out_ref.shape[0]
    peers = part_refs[0].shape[0] // 9 * 8
    blocks = key_ref.shape[0] // LANES
    heads = part_refs[0].shape[1]
    flat = heads * len(part_refs)
    queries = jnp.concatenate(
        [ref[step * sources + i] for i in range(sources) for ref in part_refs], axis=0
    )
    corner = lax.broadcasted_iota(jnp.int32, (heads, LANES), 0) == lax.broadcasted_iota(
        jnp.int32, (heads, LANES), 1
    )
    tails = [ref[peers + step // 2].astype(jnp.float32) for ref in part_refs]
    half = step % 2 == 0
    weights = []
    for i in range(sources):
        for tail in tails:
            row = jnp.where(half, tail[i : i + 1], tail[sources + i : sources + i + 1])
            column = jnp.sum(jnp.where(corner, row, 0.0), axis=1, keepdims=True)
            weights.append(jnp.broadcast_to(column, (heads, LANES)))
    for b in range(blocks // 2):
        keys = key_ref[2 * b * LANES : 2 * (b + 1) * LANES, :]
        dots = lax.dot_general(
            queries, keys, (((1,), (1,)), ((), ())), preferred_element_type=jnp.float32
        )
        for j in range(2):
            for i in range(sources):
                total = None
                for d in range(len(part_refs)):
                    at = i * flat + d * heads
                    part = (
                        jnp.maximum(dots[at : at + heads, j * LANES : (j + 1) * LANES], 0.0)
                        * weights[i * len(part_refs) + d]
                    )
                    total = part if total is None else total + part
                sum_ref[i, 2 * b + j : 2 * b + j + 1, :] = jnp.sum(total, axis=0, keepdims=True)
    for i in range(sources):
        out_ref[i] = sum_ref[i].astype(out_ref.dtype)


def index_scores(keys, parts):
    sources = 4
    peers = parts[0].shape[0] // 9 * 8
    blocks = keys.shape[0] // LANES
    return pl.pallas_call(
        score_kernel,
        grid=(peers // sources,),
        in_specs=[pl.BlockSpec(memory_space=pltpu.VMEM)] * (1 + len(parts)),
        out_specs=pl.BlockSpec((sources, blocks, LANES), lambda i: (i, 0, 0)),
        out_shape=jax.ShapeDtypeStruct((peers, blocks, LANES), jnp.bfloat16),
        scratch_shapes=[pltpu.VMEM((sources, blocks, LANES), jnp.float32)],
        compiler_params=pltpu.CompilerParams(vmem_limit_bytes=16 * MIB),
        cost_estimate=pl.CostEstimate(
            flops=2 * peers * H_IDX * keys.shape[0] * D_IDX,
            bytes_accessed=2 * MIB,
            transcendentals=0,
        ),
        name="index_scores",
    )(keys, *parts)


def attend_kernel(
    used_ref, query_ref, page_ref, rest_ref, score_ref, out_ref, logp_ref, top_ref, total_ref, sum_ref
):
    step = pl.program_id(0)
    sources = page_ref.shape[0]

    @pl.when(step == 0)
    def _():
        top_ref[...] = jnp.full_like(top_ref, NEG)
        total_ref[...] = jnp.zeros_like(total_ref)
        sum_ref[...] = jnp.zeros_like(sum_ref)
        scores = score_ref[...].astype(jnp.float32).reshape(logp_ref.shape)
        top = jnp.max(scores)
        total = jnp.sum(jnp.exp(scores - top), keepdims=True)
        logp_ref[...] = scores - (top + jnp.log(total)) + jnp.log(jnp.float32(scores.size))

    left = lax.broadcasted_iota(jnp.int32, (1, LANES), 1) < PAGE
    live = []
    for i in range(sources):
        slots = [
            jnp.where(used_ref[step * sources + i, 0, s] > 0, 0.0, NEG) for s in range(2)
        ]
        live.append(jnp.where(left, slots[0], slots[1]))
    live = jnp.concatenate(live, axis=1)
    keys = jnp.concatenate(
        [
            jnp.concatenate([page_ref[i] for i in range(sources)], axis=1),
            jnp.concatenate([rest_ref[i, : DK - FIRST] for i in range(sources)], axis=1),
        ],
        axis=0,
    )
    scale = (QK_NOPE + D_ROPE) ** (-0.5)
    logits = jnp.dot(query_ref[...], keys, preferred_element_type=jnp.float32) * scale + live
    old = top_ref[...]
    new = jnp.maximum(old, jnp.max(logits, axis=1, keepdims=True))
    fade = jnp.exp(old - new)
    top_ref[...] = new
    expo = jnp.exp(logits - new[:, :1])
    total_ref[...] = total_ref[...] * fade + jnp.sum(expo, axis=1, keepdims=True)
    mixed = lax.dot_general(
        expo.astype(jnp.bfloat16),
        keys[:D_LAT],
        (((1,), (1,)), ((), ())),
        preferred_element_type=jnp.float32,
    )
    sum_ref[...] = sum_ref[...] * fade[:, :1] + mixed

    @pl.when(step == pl.num_programs(0) - 1)
    def _():
        out_ref[...] = (sum_ref[...] / total_ref[...][:, :1]).astype(out_ref.dtype)


def attend(used, query, pages, rest):
    sources = 16
    peers = pages.shape[0]
    depth = DK - FIRST
    blocks = rest.shape[1] - depth
    tokens = peers * LANES
    return pl.pallas_call(
        attend_kernel,
        grid=(peers // sources,),
        in_specs=[
            pl.BlockSpec(memory_space=pltpu.SMEM),
            pl.BlockSpec(memory_space=pltpu.VMEM),
            pl.BlockSpec((sources, FIRST, LANES), lambda i: (i, 0, 0)),
            pl.BlockSpec((sources, depth, LANES), lambda i: (i, 0, 0)),
            pl.BlockSpec((peers, blocks, LANES), lambda i: (0, depth // blocks, 0)),
        ],
        out_specs=(
            pl.BlockSpec((H, D_LAT), lambda i: (0, 0)),
            pl.BlockSpec((peers * blocks, LANES), lambda i: (0, 0)),
        ),
        scratch_shapes=[
            pltpu.VMEM((H, LANES), jnp.float32),
            pltpu.VMEM((H, LANES), jnp.float32),
            pltpu.VMEM((H, D_LAT), jnp.float32),
        ],
        out_shape=(
            jax.ShapeDtypeStruct((H, D_LAT), jnp.bfloat16),
            jax.ShapeDtypeStruct((peers * blocks, LANES), jnp.float32),
        ),
        compiler_params=pltpu.CompilerParams(vmem_limit_bytes=40 * MIB),
        cost_estimate=pl.CostEstimate(
            flops=2 * H * tokens * (2 * D_LAT + D_ROPE),
            bytes_accessed=5 * MIB,
            transcendentals=H * tokens,
        ),
        name="attend",
    )(used, query, pages, rest, rest)


def per_device(idx_query, idx_weight, idx_keys, q_latent, latent_cache, page_ids):
    owners = lax.axis_size("ctx")
    groups = lax.axis_size("qry")
    rows = idx_weight.shape[0]
    exchange = functools.partial(
        lax.all_to_all, axis_name="ctx", split_axis=0, concat_axis=0, tiled=True
    )

    def swap(x, axis, size, bits):
        return lax.ppermute(x, axis, [(i, i ^ bits) for i in range(size)])

    cache = latent_cache.T
    sent, table = requests(page_ids, idx_query, idx_weight, owners, idx_keys.shape[0] // PAGE)
    got = exchange(sent)
    asked = got[:, rows // 2 + 1, 0, :2].astype(jnp.int32)
    packed, got = lax.optimization_barrier((pack_pages(asked, cache, 0, FIRST), got))
    pages = exchange(packed)

    place = jnp.stack([lax.axis_index("qry"), lax.axis_index("ctx") % 2]).astype(jnp.int32)
    parts = partner_parts(place, got, swap(got, "ctx", owners, 1), rows)
    parts = [parts[0]] + [swap(parts[d], "qry", groups, d) for d in range(1, groups)]
    scores = index_scores(idx_keys, parts)
    rest = pack_pages(asked, cache, FIRST, DK - FIRST, scores)
    latent = q_latent.reshape(H, DK)
    rest, pages, latent = lax.optimization_barrier((rest, pages, latent))
    rest = exchange(rest)

    latent_out, index_logp = attend(table, latent, pages, rest)
    return (index_logp.reshape(1, -1), latent_out.reshape(1, -1))


def solution(mesh):
    in_specs = (
        P("ctx", "qry"),
        P("ctx", "qry"),
        P("ctx", None),
        P(("ctx", "qry"), None),
        P("ctx", None),
        P(("ctx", "qry"), None),
    )
    out_specs = (P(("ctx", "qry"), None), P(("ctx", "qry"), None))
    return jax.shard_map(
        per_device, mesh=mesh, in_specs=in_specs, out_specs=out_specs, check_vma=False
    )
```

```python
import functools

import jax
import jax.numpy as jnp
from jax import lax
from jax.experimental import pallas as pl
from jax.experimental.pallas import tpu as pltpu
from jax.sharding import PartitionSpec as P

H_IDX = 64
D_IDX = 128
H = 128
D_LAT = 512
D_ROPE = 64
DK = D_LAT + D_ROPE
QK_NOPE = 128
PAGE = 64
TOPP = 32
LANES = 128
NEG = -1e30
FIRST = 384
MIB = 1 << 20


def request_kernel(pages_dev, ids_ref, query_ref, weight_ref, out_ref, table_ref, turn_ref):
    owners = out_ref.shape[0]
    rows, heads = weight_ref.shape
    part = rows // 2
    ids = ids_ref[...]
    owner, local = ids // pages_dev, ids % pages_dev
    mine = owner == lax.broadcasted_iota(jnp.int32, (owners, TOPP), 0)
    low = jnp.min(jnp.where(mine, local, pages_dev), axis=1, keepdims=True)
    high = jnp.max(jnp.where(mine, local, -1), axis=1, keepdims=True)
    turn = (low < high) & (low % 2 == 1) & (high % 2 == 0)
    first = jnp.where(turn, high, low)
    second = jnp.where(turn, low, high)
    single = low == high
    left = jnp.where((high < 0) | (single & (low % 2 == 1)), 0, first + 1)
    right = jnp.where((high < 0) | (single & (low % 2 == 0)), 0, second + 1)
    lane = lax.broadcasted_iota(jnp.int32, (owners, LANES), 1)
    table = jnp.where(lane == 0, left, jnp.where(lane == 1, right, 0)).reshape(owners, 1, LANES)
    table_ref[...] = table
    weight = jnp.concatenate(
        [weight_ref[...].astype(jnp.float32), jnp.zeros((rows, LANES - heads), jnp.float32)], axis=1
    )
    asked = jnp.broadcast_to(table.astype(jnp.float32), (owners, rows, LANES))
    for h in range(heads):
        turn_ref[pl.ds(h, rows, stride=heads), :] = query_ref[
            :, h * LANES : (h + 1) * LANES
        ].astype(jnp.float32)
    query = turn_ref[...].astype(out_ref.dtype).reshape(rows, heads, LANES)
    for t in range(owners):
        out_ref[t, :part] = query[t % 2 * part : (t % 2 + 1) * part]
    out_ref[:, part] = jnp.broadcast_to(weight[None], (owners, rows, LANES)).astype(out_ref.dtype)
    out_ref[:, part + 1] = asked.astype(out_ref.dtype)


def requests(page_ids, query, weight, owners, pages_dev):
    rows, heads = weight.shape
    return pl.pallas_call(
        functools.partial(request_kernel, pages_dev),
        out_shape=(
            pltpu.HBM((owners, rows // 2 + 2, heads, LANES), query.dtype),
            jax.ShapeDtypeStruct((owners, 1, LANES), jnp.int32),
        ),
        scratch_shapes=[pltpu.VMEM((rows * heads, LANES), jnp.float32)],
        name="requests",
    )(page_ids, query, weight)


def stage_kernel(cache_hbm, out_ref, sem):
    load = pltpu.make_async_copy(cache_hbm, out_ref, sem)
    load.start()
    load.wait()


def stage(cache):
    return pl.pallas_call(
        stage_kernel,
        in_specs=[pl.BlockSpec(memory_space=pltpu.HBM)],
        out_specs=pl.BlockSpec(memory_space=pltpu.VMEM),
        out_shape=pltpu.VMEM(cache.shape, cache.dtype),
        scratch_shapes=[pltpu.SemaphoreType.DMA],
        compiler_params=pltpu.CompilerParams(vmem_limit_bytes=60 * MIB),
        cost_estimate=pl.CostEstimate(flops=0, bytes_accessed=5 * MIB, transcendentals=0),
        name="stage",
    )(cache)


GROUP = 4


def pack_kernel(first_row, depth, table_ref, cache_ref, *refs):
    score_refs, (out_hbm, stage_ref, out_sems) = refs[:-3], refs[-3:]
    peers = stage_ref.shape[0]
    rows = slice(first_row, first_row + depth)
    for score_ref in score_refs:
        stage_ref[:, depth:, :] = score_ref[...]
    left = lax.broadcasted_iota(jnp.int32, (depth, LANES), 1) < PAGE

    def tile(page):
        return cache_ref[rows, pl.ds(pl.multiple_of(page // 2 * LANES, LANES), LANES)]

    def turned(x):
        return jnp.concatenate([x[:, PAGE:], x[:, :PAGE]], axis=1)

    def send(g):
        peer = pl.ds(g * GROUP, GROUP)
        return pltpu.make_async_copy(stage_ref.at[peer], out_hbm.at[peer], out_sems.at[g])

    for r in range(peers):
        first = table_ref[r, 0]
        second = table_ref[r, 1]
        first = jnp.where(first > 0, first - 1, 0)
        second = jnp.where(second > 0, second - 1, 1)
        straight = (first % 2 == 0) & (second % 2 == 1)

        @pl.when(straight)
        def _(r=r, first=first, second=second):
            stage_ref[r, :depth] = jnp.where(left, tile(first), tile(second))

        @pl.when(jnp.logical_not(straight))
        def _(r=r, first=first, second=second):
            a, b = tile(first), tile(second)
            a = jnp.where(first % 2 == 0, a, turned(a))
            b = jnp.where(second % 2 == 1, b, turned(b))
            stage_ref[r, :depth] = jnp.where(left, a, b)

        if r % GROUP == GROUP - 1:
            send(r // GROUP).start()
    for g in range(peers // GROUP):
        send(g).wait()


def pack_pages(table, cache, first_row, depth, *scores):
    peers = table.shape[0]
    length = depth + sum(s.shape[1] for s in scores)
    return pl.pallas_call(
        functools.partial(pack_kernel, first_row, depth),
        in_specs=[
            pl.BlockSpec(memory_space=pltpu.SMEM),
            pl.BlockSpec(memory_space=pltpu.VMEM),
        ]
        + [pl.BlockSpec(memory_space=pltpu.VMEM)] * len(scores),
        out_specs=pl.BlockSpec(memory_space=pltpu.HBM),
        out_shape=pltpu.HBM((peers, length, LANES), cache.dtype),
        scratch_shapes=[
            pltpu.VMEM((peers, length, LANES), cache.dtype),
            pltpu.SemaphoreType.DMA((peers // GROUP,)),
        ],
        compiler_params=pltpu.CompilerParams(vmem_limit_bytes=24 * MIB),
        cost_estimate=pl.CostEstimate(flops=0, bytes_accessed=8 * MIB, transcendentals=0),
        name="pack_pages",
    )(table, cache, *scores)


def partner_kernel(place_ref, got_ref, other_ref, *out_refs):
    peers, part = got_ref.shape[0], got_ref.shape[1] - 2
    weights = got_ref[:, part].astype(jnp.float32)
    place = lax.broadcasted_iota(jnp.int32, weights.shape, 1)
    for d, out_ref in enumerate(out_refs):
        row = place_ref[0] ^ d
        mine = row // part == place_ref[1]

        @pl.when(mine)
        def _(out_ref=out_ref, row=row):
            out_ref[:peers] = got_ref[:, row % part]

        @pl.when(jnp.logical_not(mine))
        def _(out_ref=out_ref, row=row):
            out_ref[:peers] = other_ref[:, row % part]

        weight = jnp.sum(jnp.where(place == row, weights, 0.0), axis=1)
        out_ref[peers:] = weight.reshape(peers // 8, 8, LANES).astype(out_ref.dtype)


def partner_parts(place, got, other, rows):
    peers, _, heads, _ = got.shape
    part = jax.ShapeDtypeStruct((peers + peers // 8, heads, LANES), got.dtype)
    return pl.pallas_call(
        partner_kernel,
        in_specs=[
            pl.BlockSpec(memory_space=pltpu.SMEM),
            pl.BlockSpec(memory_space=pltpu.VMEM),
            pl.BlockSpec(memory_space=pltpu.VMEM),
        ],
        out_shape=(part,) * rows,
        compiler_params=pltpu.CompilerParams(vmem_limit_bytes=16 * MIB),
        cost_estimate=pl.CostEstimate(flops=0, bytes_accessed=2 * MIB, transcendentals=0),
        name="partner_parts",
    )(place, got, other)


def score_kernel(key_ref, *refs):
    part_refs, (out_ref, sum_ref) = refs[:-2], refs[-2:]
    step = pl.program_id(0)
    sources = out_ref.shape[0]
    peers = part_refs[0].shape[0] // 9 * 8
    blocks = key_ref.shape[0] // LANES
    heads = part_refs[0].shape[1]
    flat = heads * len(part_refs)
    queries = jnp.concatenate(
        [ref[step * sources + i] for i in range(sources) for ref in part_refs], axis=0
    )
    corner = lax.broadcasted_iota(jnp.int32, (heads, LANES), 0) == lax.broadcasted_iota(
        jnp.int32, (heads, LANES), 1
    )
    tails = [ref[peers + step // 2].astype(jnp.float32) for ref in part_refs]
    half = step % 2 == 0
    weights = []
    for i in range(sources):
        for tail in tails:
            row = jnp.where(half, tail[i : i + 1], tail[sources + i : sources + i + 1])
            column = jnp.sum(jnp.where(corner, row, 0.0), axis=1, keepdims=True)
            weights.append(jnp.broadcast_to(column, (heads, LANES)))
    for b in range(blocks // 2):
        keys = key_ref[2 * b * LANES : 2 * (b + 1) * LANES, :]
        dots = lax.dot_general(
            queries, keys, (((1,), (1,)), ((), ())), preferred_element_type=jnp.float32
        )
        for j in range(2):
            for i in range(sources):
                total = None
                for d in range(len(part_refs)):
                    at = i * flat + d * heads
                    part = (
                        jnp.maximum(dots[at : at + heads, j * LANES : (j + 1) * LANES], 0.0)
                        * weights[i * len(part_refs) + d]
                    )
                    total = part if total is None else total + part
                sum_ref[i, 2 * b + j : 2 * b + j + 1, :] = jnp.sum(total, axis=0, keepdims=True)
    for i in range(sources):
        out_ref[i] = sum_ref[i].astype(out_ref.dtype)


def index_scores(keys, parts):
    sources = 4
    peers = parts[0].shape[0] // 9 * 8
    blocks = keys.shape[0] // LANES
    return pl.pallas_call(
        score_kernel,
        grid=(peers // sources,),
        in_specs=[pl.BlockSpec(memory_space=pltpu.VMEM)] * (1 + len(parts)),
        out_specs=pl.BlockSpec((sources, blocks, LANES), lambda i: (i, 0, 0)),
        out_shape=jax.ShapeDtypeStruct((peers, blocks, LANES), jnp.bfloat16),
        scratch_shapes=[pltpu.VMEM((sources, blocks, LANES), jnp.float32)],
        compiler_params=pltpu.CompilerParams(vmem_limit_bytes=16 * MIB),
        cost_estimate=pl.CostEstimate(
            flops=2 * peers * H_IDX * keys.shape[0] * D_IDX,
            bytes_accessed=2 * MIB,
            transcendentals=0,
        ),
        name="index_scores",
    )(keys, *parts)


def attend_kernel(
    used_ref, query_ref, page_ref, rest_ref, score_ref, out_ref, logp_ref, top_ref, total_ref, sum_ref
):
    step = pl.program_id(0)
    sources = page_ref.shape[0]

    @pl.when(step == 0)
    def _():
        top_ref[...] = jnp.full_like(top_ref, NEG)
        total_ref[...] = jnp.zeros_like(total_ref)
        sum_ref[...] = jnp.zeros_like(sum_ref)
        scores = score_ref[...].astype(jnp.float32).reshape(logp_ref.shape)
        top = jnp.max(scores)
        total = jnp.sum(jnp.exp(scores - top), keepdims=True)
        logp_ref[...] = scores - (top + jnp.log(total)) + jnp.log(jnp.float32(scores.size))

    left = lax.broadcasted_iota(jnp.int32, (1, LANES), 1) < PAGE
    live = []
    for i in range(sources):
        slots = [
            jnp.where(used_ref[step * sources + i, 0, s] > 0, 0.0, NEG) for s in range(2)
        ]
        live.append(jnp.where(left, slots[0], slots[1]))
    live = jnp.concatenate(live, axis=1)
    keys = jnp.concatenate(
        [
            jnp.concatenate([page_ref[i] for i in range(sources)], axis=1),
            jnp.concatenate([rest_ref[i, : DK - FIRST] for i in range(sources)], axis=1),
        ],
        axis=0,
    )
    scale = (QK_NOPE + D_ROPE) ** (-0.5)
    logits = jnp.dot(query_ref[...], keys, preferred_element_type=jnp.float32) * scale + live
    old = top_ref[...]
    new = jnp.maximum(old, jnp.max(logits, axis=1, keepdims=True))
    fade = jnp.exp(old - new)
    top_ref[...] = new
    expo = jnp.exp(logits - new[:, :1])
    total_ref[...] = total_ref[...] * fade + jnp.sum(expo, axis=1, keepdims=True)
    mixed = lax.dot_general(
        expo.astype(jnp.bfloat16),
        keys[:D_LAT],
        (((1,), (1,)), ((), ())),
        preferred_element_type=jnp.float32,
    )
    sum_ref[...] = sum_ref[...] * fade[:, :1] + mixed

    @pl.when(step == pl.num_programs(0) - 1)
    def _():
        out_ref[...] = (sum_ref[...] / total_ref[...][:, :1]).astype(out_ref.dtype)


def attend(used, query, pages, rest):
    sources = 16
    peers = pages.shape[0]
    depth = DK - FIRST
    blocks = rest.shape[1] - depth
    tokens = peers * LANES
    return pl.pallas_call(
        attend_kernel,
        grid=(peers // sources,),
        in_specs=[
            pl.BlockSpec(memory_space=pltpu.SMEM),
            pl.BlockSpec(memory_space=pltpu.VMEM),
            pl.BlockSpec((sources, FIRST, LANES), lambda i: (i, 0, 0)),
            pl.BlockSpec((sources, depth, LANES), lambda i: (i, 0, 0)),
            pl.BlockSpec((peers, blocks, LANES), lambda i: (0, depth // blocks, 0)),
        ],
        out_specs=(
            pl.BlockSpec((H, D_LAT), lambda i: (0, 0)),
            pl.BlockSpec((peers * blocks, LANES), lambda i: (0, 0)),
        ),
        scratch_shapes=[
            pltpu.VMEM((H, LANES), jnp.float32),
            pltpu.VMEM((H, LANES), jnp.float32),
            pltpu.VMEM((H, D_LAT), jnp.float32),
        ],
        out_shape=(
            jax.ShapeDtypeStruct((H, D_LAT), jnp.bfloat16),
            jax.ShapeDtypeStruct((peers * blocks, LANES), jnp.float32),
        ),
        compiler_params=pltpu.CompilerParams(vmem_limit_bytes=40 * MIB),
        cost_estimate=pl.CostEstimate(
            flops=2 * H * tokens * (2 * D_LAT + D_ROPE),
            bytes_accessed=5 * MIB,
            transcendentals=H * tokens,
        ),
        name="attend",
    )(used, query, pages, rest, rest)


def per_device(idx_query, idx_weight, idx_keys, q_latent, latent_cache, page_ids):
    owners = lax.axis_size("ctx")
    groups = lax.axis_size("qry")
    rows = idx_weight.shape[0]
    exchange = functools.partial(
        lax.all_to_all, axis_name="ctx", split_axis=0, concat_axis=0, tiled=True
    )

    def swap(x, axis, size, bits):
        return lax.ppermute(x, axis, [(i, i ^ bits) for i in range(size)])

    sent, table = requests(page_ids, idx_query, idx_weight, owners, idx_keys.shape[0] // PAGE)
    got, latent, cache = lax.optimization_barrier(
        (exchange(sent), q_latent.reshape(H, DK), stage(latent_cache.T))
    )
    asked = got[:, rows // 2 + 1, 0, :2].astype(jnp.int32)
    packed, got = lax.optimization_barrier((pack_pages(asked, cache, 0, FIRST), got))
    pages = exchange(packed)

    place = jnp.stack([lax.axis_index("qry"), lax.axis_index("ctx") % 2]).astype(jnp.int32)
    parts = partner_parts(place, got, swap(got, "ctx", owners, 1), rows)
    parts = [parts[0]] + [swap(parts[d], "qry", groups, d) for d in range(1, groups)]
    scores = index_scores(idx_keys, parts)
    rest = pack_pages(asked, cache, FIRST, DK - FIRST, scores)
    rest, pages = lax.optimization_barrier((rest, pages))
    rest = exchange(rest)

    latent_out, index_logp = attend(table, latent, pages, rest)
    return (index_logp.reshape(1, -1), latent_out.reshape(1, -1))


def solution(mesh):
    in_specs = (
        P("ctx", "qry"),
        P("ctx", "qry"),
        P("ctx", None),
        P(("ctx", "qry"), None),
        P("ctx", None),
        P(("ctx", "qry"), None),
    )
    out_specs = (P(("ctx", "qry"), None), P(("ctx", "qry"), None))
    return jax.shard_map(
        per_device, mesh=mesh, in_specs=in_specs, out_specs=out_specs, check_vma=False
    )
```

```python
import functools

import jax
import jax.numpy as jnp
from jax import lax
from jax.experimental import pallas as pl
from jax.experimental.pallas import tpu as pltpu
from jax.sharding import PartitionSpec as P

H_IDX = 64
D_IDX = 128
H = 128
D_LAT = 512
D_ROPE = 64
DK = D_LAT + D_ROPE
QK_NOPE = 128
PAGE = 64
TOPP = 32
LANES = 128
NEG = -1e30
MIB = 1 << 20


def request_kernel(pages_dev, ids_ref, query_ref, weight_ref, out_ref, table_ref, turn_ref):
    owners = out_ref.shape[0]
    rows, heads = weight_ref.shape
    part = rows // 2
    ids = ids_ref[...]
    owner, local = ids // pages_dev, ids % pages_dev
    mine = owner == lax.broadcasted_iota(jnp.int32, (owners, TOPP), 0)
    low = jnp.min(jnp.where(mine, local, pages_dev), axis=1, keepdims=True)
    high = jnp.max(jnp.where(mine, local, -1), axis=1, keepdims=True)
    turn = (low < high) & (low % 2 == 1) & (high % 2 == 0)
    first = jnp.where(turn, high, low)
    second = jnp.where(turn, low, high)
    single = low == high
    left = jnp.where((high < 0) | (single & (low % 2 == 1)), 0, first + 1)
    right = jnp.where((high < 0) | (single & (low % 2 == 0)), 0, second + 1)
    lane = lax.broadcasted_iota(jnp.int32, (owners, LANES), 1)
    table = jnp.where(lane == 0, left, jnp.where(lane == 1, right, 0)).reshape(owners, 1, LANES)
    table_ref[...] = table
    weight = jnp.concatenate(
        [weight_ref[...].astype(jnp.float32), jnp.zeros((rows, LANES - heads), jnp.float32)], axis=1
    )
    asked = jnp.where(lane == heads, left, jnp.where(lane == heads + 1, right, 0))
    asked = asked.astype(jnp.float32).reshape(owners, 1, LANES)
    for h in range(heads):
        turn_ref[pl.ds(h, rows, stride=heads), :] = query_ref[
            :, h * LANES : (h + 1) * LANES
        ].astype(jnp.float32)
    query = turn_ref[...].astype(out_ref.dtype).reshape(rows, heads, LANES)
    for t in range(owners):
        out_ref[t, :part] = query[t % 2 * part : (t % 2 + 1) * part]
    out_ref[:, part] = (weight[None] + asked).astype(out_ref.dtype)


def requests(page_ids, query, weight, owners, pages_dev):
    rows, heads = weight.shape
    return pl.pallas_call(
        functools.partial(request_kernel, pages_dev),
        out_shape=(
            pltpu.HBM((owners, rows // 2 + 1, heads, LANES), query.dtype),
            jax.ShapeDtypeStruct((owners, 1, LANES), jnp.int32),
        ),
        scratch_shapes=[pltpu.VMEM((rows * heads, LANES), jnp.float32)],
        name="requests",
    )(page_ids, query, weight)


def stage_kernel(cache_hbm, out_ref, sem):
    load = pltpu.make_async_copy(cache_hbm, out_ref, sem)
    load.start()
    load.wait()


def stage(cache):
    return pl.pallas_call(
        stage_kernel,
        in_specs=[pl.BlockSpec(memory_space=pltpu.HBM)],
        out_specs=pl.BlockSpec(memory_space=pltpu.VMEM),
        out_shape=pltpu.VMEM(cache.shape, cache.dtype),
        scratch_shapes=[pltpu.SemaphoreType.DMA],
        compiler_params=pltpu.CompilerParams(vmem_limit_bytes=60 * MIB),
        cost_estimate=pl.CostEstimate(flops=0, bytes_accessed=5 * MIB, transcendentals=0),
        name="stage",
    )(cache)


GROUP = 4


def pack_kernel(table_ref, cache_ref, out_hbm, stage_ref, out_sems):
    peers = stage_ref.shape[0]
    left = lax.broadcasted_iota(jnp.int32, (DK, LANES), 1) < PAGE

    def tile(page):
        return cache_ref[:, pl.ds(pl.multiple_of(page // 2 * LANES, LANES), LANES)]

    def turned(x):
        return jnp.concatenate([x[:, PAGE:], x[:, :PAGE]], axis=1)

    def send(g):
        peer = pl.ds(g * GROUP, GROUP)
        return pltpu.make_async_copy(stage_ref.at[peer], out_hbm.at[peer], out_sems.at[g])

    for r in range(peers):
        first = table_ref[r, 0]
        second = table_ref[r, 1]
        first = jnp.where(first > 0, first - 1, 0)
        second = jnp.where(second > 0, second - 1, 1)
        straight = (first % 2 == 0) & (second % 2 == 1)

        @pl.when(straight)
        def _(r=r, first=first, second=second):
            stage_ref[r] = jnp.where(left, tile(first), tile(second))

        @pl.when(jnp.logical_not(straight))
        def _(r=r, first=first, second=second):
            a, b = tile(first), tile(second)
            a = jnp.where(first % 2 == 0, a, turned(a))
            b = jnp.where(second % 2 == 1, b, turned(b))
            stage_ref[r] = jnp.where(left, a, b)

        if r % GROUP == GROUP - 1:
            send(r // GROUP).start()
    for g in range(peers // GROUP):
        send(g).wait()


def pack_pages(table, cache):
    peers = table.shape[0]
    return pl.pallas_call(
        pack_kernel,
        in_specs=[
            pl.BlockSpec(memory_space=pltpu.SMEM),
            pl.BlockSpec(memory_space=pltpu.VMEM),
        ],
        out_specs=pl.BlockSpec(memory_space=pltpu.HBM),
        out_shape=pltpu.HBM((peers, DK, LANES), cache.dtype),
        scratch_shapes=[
            pltpu.VMEM((peers, DK, LANES), cache.dtype),
            pltpu.SemaphoreType.DMA((peers // GROUP,)),
        ],
        compiler_params=pltpu.CompilerParams(vmem_limit_bytes=24 * MIB),
        cost_estimate=pl.CostEstimate(flops=0, bytes_accessed=8 * MIB, transcendentals=0),
        name="pack_pages",
    )(table, cache)


def partner_kernel(place_ref, got_ref, other_ref, *out_refs):
    peers, part = got_ref.shape[0], got_ref.shape[1] - 1
    weights = got_ref[:, part].astype(jnp.float32)
    place = lax.broadcasted_iota(jnp.int32, weights.shape, 1)
    for d, out_ref in enumerate(out_refs):
        row = place_ref[0] ^ d
        mine = row // part == place_ref[1]

        @pl.when(mine)
        def _(out_ref=out_ref, row=row):
            out_ref[:peers] = got_ref[:, row % part]

        @pl.when(jnp.logical_not(mine))
        def _(out_ref=out_ref, row=row):
            out_ref[:peers] = other_ref[:, row % part]

        weight = jnp.sum(jnp.where(place == row, weights, 0.0), axis=1)
        out_ref[peers:] = weight.reshape(peers // 8, 8, LANES).astype(out_ref.dtype)


def partner_parts(place, got, other, rows):
    peers, _, heads, _ = got.shape
    part = jax.ShapeDtypeStruct((peers + peers // 8, heads, LANES), got.dtype)
    return pl.pallas_call(
        partner_kernel,
        in_specs=[
            pl.BlockSpec(memory_space=pltpu.SMEM),
            pl.BlockSpec(memory_space=pltpu.VMEM),
            pl.BlockSpec(memory_space=pltpu.VMEM),
        ],
        out_shape=(part,) * rows,
        compiler_params=pltpu.CompilerParams(vmem_limit_bytes=16 * MIB),
        cost_estimate=pl.CostEstimate(flops=0, bytes_accessed=2 * MIB, transcendentals=0),
        name="partner_parts",
    )(place, got, other)


def score_kernel(key_ref, *refs):
    part_refs, (out_ref, sum_ref) = refs[:-2], refs[-2:]
    step = pl.program_id(0)
    sources = out_ref.shape[0]
    peers = part_refs[0].shape[0] // 9 * 8
    blocks = key_ref.shape[0] // LANES
    heads = part_refs[0].shape[1]
    flat = heads * len(part_refs)
    queries = jnp.concatenate(
        [ref[step * sources + i] for i in range(sources) for ref in part_refs], axis=0
    )
    corner = lax.broadcasted_iota(jnp.int32, (heads, LANES), 0) == lax.broadcasted_iota(
        jnp.int32, (heads, LANES), 1
    )
    tails = [ref[peers + step // 2].astype(jnp.float32) for ref in part_refs]
    half = step % 2 == 0
    weights = []
    for i in range(sources):
        for tail in tails:
            row = jnp.where(half, tail[i : i + 1], tail[sources + i : sources + i + 1])
            column = jnp.sum(jnp.where(corner, row, 0.0), axis=1, keepdims=True)
            weights.append(jnp.broadcast_to(column, (heads, LANES)))
    for b in range(blocks // 2):
        keys = key_ref[2 * b * LANES : 2 * (b + 1) * LANES, :]
        dots = lax.dot_general(
            queries, keys, (((1,), (1,)), ((), ())), preferred_element_type=jnp.float32
        )
        for j in range(2):
            for i in range(sources):
                total = None
                for d in range(len(part_refs)):
                    at = i * flat + d * heads
                    part = (
                        jnp.maximum(dots[at : at + heads, j * LANES : (j + 1) * LANES], 0.0)
                        * weights[i * len(part_refs) + d]
                    )
                    total = part if total is None else total + part
                sum_ref[i, 2 * b + j : 2 * b + j + 1, :] = jnp.sum(total, axis=0, keepdims=True)
    for i in range(sources):
        out_ref[i] = sum_ref[i].astype(out_ref.dtype)


def index_scores(keys, parts):
    sources = 4
    peers = parts[0].shape[0] // 9 * 8
    blocks = keys.shape[0] // LANES
    return pl.pallas_call(
        score_kernel,
        grid=(peers // sources,),
        in_specs=[pl.BlockSpec(memory_space=pltpu.VMEM)] * (1 + len(parts)),
        out_specs=pl.BlockSpec((sources, blocks, LANES), lambda i: (i, 0, 0)),
        out_shape=jax.ShapeDtypeStruct((peers, blocks, LANES), jnp.bfloat16),
        scratch_shapes=[pltpu.VMEM((sources, blocks, LANES), jnp.float32)],
        compiler_params=pltpu.CompilerParams(vmem_limit_bytes=16 * MIB),
        cost_estimate=pl.CostEstimate(
            flops=2 * peers * H_IDX * keys.shape[0] * D_IDX,
            bytes_accessed=2 * MIB,
            transcendentals=0,
        ),
        name="index_scores",
    )(keys, *parts)


def logp_kernel(score_ref, out_ref):
    scores = score_ref[...].astype(jnp.float32)
    top = jnp.max(scores)
    total = jnp.sum(jnp.exp(scores - top), keepdims=True)
    out_ref[...] = scores - (top + jnp.log(total)) + jnp.log(jnp.float32(scores.size))


def log_distribution(scores):
    return pl.pallas_call(
        logp_kernel,
        out_shape=jax.ShapeDtypeStruct(scores.shape, jnp.float32),
        compiler_params=pltpu.CompilerParams(vmem_limit_bytes=8 * MIB),
        cost_estimate=pl.CostEstimate(
            flops=4 * scores.size, bytes_accessed=6 * scores.size, transcendentals=scores.size
        ),
        name="log_distribution",
    )(scores)


def attend_kernel(used_ref, query_ref, page_ref, out_ref, top_ref, total_ref, sum_ref):
    step = pl.program_id(0)
    sources = page_ref.shape[0]

    @pl.when(step == 0)
    def _():
        top_ref[...] = jnp.full_like(top_ref, NEG)
        total_ref[...] = jnp.zeros_like(total_ref)
        sum_ref[...] = jnp.zeros_like(sum_ref)

    left = lax.broadcasted_iota(jnp.int32, (1, LANES), 1) < PAGE
    live = []
    for i in range(sources):
        slots = [
            jnp.where(used_ref[step * sources + i, 0, s] > 0, 0.0, NEG) for s in range(2)
        ]
        live.append(jnp.where(left, slots[0], slots[1]))
    live = jnp.concatenate(live, axis=1)
    keys = jnp.concatenate([page_ref[i] for i in range(sources)], axis=1)
    scale = (QK_NOPE + D_ROPE) ** (-0.5)
    logits = jnp.dot(query_ref[...], keys, preferred_element_type=jnp.float32) * scale + live
    old = top_ref[...]
    new = jnp.maximum(old, jnp.max(logits, axis=1, keepdims=True))
    fade = jnp.exp(old - new)
    top_ref[...] = new
    expo = jnp.exp(logits - new[:, :1])
    total_ref[...] = total_ref[...] * fade + jnp.sum(expo, axis=1, keepdims=True)
    mixed = lax.dot_general(
        expo.astype(jnp.bfloat16),
        keys[:D_LAT],
        (((1,), (1,)), ((), ())),
        preferred_element_type=jnp.float32,
    )
    sum_ref[...] = sum_ref[...] * fade[:, :1] + mixed

    @pl.when(step == pl.num_programs(0) - 1)
    def _():
        out_ref[...] = (sum_ref[...] / total_ref[...][:, :1]).astype(out_ref.dtype)


def attend(used, query, pages):
    sources = 16
    peers = pages.shape[0]
    tokens = peers * LANES
    return pl.pallas_call(
        attend_kernel,
        grid=(peers // sources,),
        in_specs=[
            pl.BlockSpec(memory_space=pltpu.SMEM),
            pl.BlockSpec(memory_space=pltpu.VMEM),
            pl.BlockSpec((sources, DK, LANES), lambda i: (i, 0, 0)),
        ],
        out_specs=pl.BlockSpec((H, D_LAT), lambda i: (0, 0)),
        scratch_shapes=[
            pltpu.VMEM((H, LANES), jnp.float32),
            pltpu.VMEM((H, LANES), jnp.float32),
            pltpu.VMEM((H, D_LAT), jnp.float32),
        ],
        out_shape=jax.ShapeDtypeStruct((H, D_LAT), jnp.bfloat16),
        compiler_params=pltpu.CompilerParams(vmem_limit_bytes=40 * MIB),
        cost_estimate=pl.CostEstimate(
            flops=2 * H * tokens * (2 * D_LAT + D_ROPE),
            bytes_accessed=5 * MIB,
            transcendentals=H * tokens,
        ),
        name="attend",
    )(used, query, pages)


def per_device(idx_query, idx_weight, idx_keys, q_latent, latent_cache, page_ids):
    owners = lax.axis_size("ctx")
    groups = lax.axis_size("qry")
    rows = idx_weight.shape[0]
    exchange = functools.partial(
        lax.all_to_all, axis_name="ctx", split_axis=0, concat_axis=0, tiled=True
    )

    def swap(x, axis, size, bits):
        return lax.ppermute(x, axis, [(i, i ^ bits) for i in range(size)])

    sent, table = requests(page_ids, idx_query, idx_weight, owners, idx_keys.shape[0] // PAGE)
    got, latent, cache = lax.optimization_barrier(
        (exchange(sent), q_latent.reshape(H, DK), stage(latent_cache.T))
    )
    heads = idx_weight.shape[1]
    asked = got[:, rows // 2, 0, heads : heads + 2].astype(jnp.int32)
    packed, got = lax.optimization_barrier((pack_pages(asked, cache), got))
    pages = exchange(packed)

    place = jnp.stack([lax.axis_index("qry"), lax.axis_index("ctx") % 2]).astype(jnp.int32)
    parts = partner_parts(place, got, swap(got, "ctx", owners, 1), rows)
    parts = [parts[0]] + [swap(parts[d], "qry", groups, d) for d in range(1, groups)]
    scores = index_scores(idx_keys, parts)
    scores, pages = lax.optimization_barrier((scores, pages))
    scores = exchange(scores)

    latent_out = attend(table, latent, pages)
    index_logp = log_distribution(scores.reshape(-1, LANES))
    return (index_logp.reshape(1, -1), latent_out.reshape(1, -1))


def solution(mesh):
    in_specs = (
        P("ctx", "qry"),
        P("ctx", "qry"),
        P("ctx", None),
        P(("ctx", "qry"), None),
        P("ctx", None),
        P(("ctx", "qry"), None),
    )
    out_specs = (P(("ctx", "qry"), None), P(("ctx", "qry"), None))
    return jax.shard_map(
        per_device, mesh=mesh, in_specs=in_specs, out_specs=out_specs, check_vma=False
    )
```

```python
import functools

import jax
import jax.numpy as jnp
from jax import lax
from jax.experimental import pallas as pl
from jax.experimental.pallas import tpu as pltpu
from jax.sharding import PartitionSpec as P

H_IDX = 64
D_IDX = 128
H = 128
D_LAT = 512
D_ROPE = 64
DK = D_LAT + D_ROPE
QK_NOPE = 128
PAGE = 64
TOPP = 32
LANES = 128
NEG = -1e30
MIB = 1 << 20


def request_kernel(pages_dev, ids_ref, query_ref, weight_ref, out_ref, table_ref, turn_ref):
    owners = out_ref.shape[0]
    rows, heads = weight_ref.shape
    part = rows // 2
    ids = ids_ref[...]
    owner, local = ids // pages_dev, ids % pages_dev
    mine = owner == lax.broadcasted_iota(jnp.int32, (owners, TOPP), 0)
    low = jnp.min(jnp.where(mine, local, pages_dev), axis=1, keepdims=True)
    high = jnp.max(jnp.where(mine, local, -1), axis=1, keepdims=True)
    turn = (low < high) & (low % 2 == 1) & (high % 2 == 0)
    first = jnp.where(turn, high, low)
    second = jnp.where(turn, low, high)
    single = low == high
    left = jnp.where((high < 0) | (single & (low % 2 == 1)), 0, first + 1)
    right = jnp.where((high < 0) | (single & (low % 2 == 0)), 0, second + 1)
    lane = lax.broadcasted_iota(jnp.int32, (owners, LANES), 1)
    table = jnp.where(lane == 0, left, jnp.where(lane == 1, right, 0)).reshape(owners, 1, LANES)
    table_ref[...] = table
    weight = jnp.concatenate(
        [weight_ref[...].astype(jnp.float32), jnp.zeros((rows, LANES - heads), jnp.float32)], axis=1
    )
    asked = jnp.where(lane == heads, left, jnp.where(lane == heads + 1, right, 0))
    asked = asked.astype(jnp.float32).reshape(owners, 1, LANES)
    for h in range(heads):
        turn_ref[pl.ds(h, rows, stride=heads), :] = query_ref[
            :, h * LANES : (h + 1) * LANES
        ].astype(jnp.float32)
    query = turn_ref[...].astype(out_ref.dtype).reshape(rows, heads, LANES)
    for t in range(owners):
        out_ref[t, :part] = query[t % 2 * part : (t % 2 + 1) * part]
    out_ref[:, part] = (weight[None] + asked).astype(out_ref.dtype)


def requests(page_ids, query, weight, owners, pages_dev):
    rows, heads = weight.shape
    return pl.pallas_call(
        functools.partial(request_kernel, pages_dev),
        out_shape=(
            pltpu.HBM((owners, rows // 2 + 1, heads, LANES), query.dtype),
            jax.ShapeDtypeStruct((owners, 1, LANES), jnp.int32),
        ),
        scratch_shapes=[pltpu.VMEM((rows * heads, LANES), jnp.float32)],
        name="requests",
    )(page_ids, query, weight)


def stage_kernel(cache_hbm, out_ref, sem):
    load = pltpu.make_async_copy(cache_hbm, out_ref, sem)
    load.start()
    load.wait()


def stage(cache):
    return pl.pallas_call(
        stage_kernel,
        in_specs=[pl.BlockSpec(memory_space=pltpu.HBM)],
        out_specs=pl.BlockSpec(memory_space=pltpu.VMEM),
        out_shape=pltpu.VMEM(cache.shape, cache.dtype),
        scratch_shapes=[pltpu.SemaphoreType.DMA],
        compiler_params=pltpu.CompilerParams(vmem_limit_bytes=60 * MIB),
        cost_estimate=pl.CostEstimate(flops=0, bytes_accessed=5 * MIB, transcendentals=0),
        name="stage",
    )(cache)


GROUP = 4


def pack_kernel(table_ref, cache_ref, out_hbm, stage_ref, out_sems):
    peers = stage_ref.shape[0]
    left = lax.broadcasted_iota(jnp.int32, (DK, LANES), 1) < PAGE

    def tile(page):
        return cache_ref[:, pl.ds(pl.multiple_of(page // 2 * LANES, LANES), LANES)]

    def turned(x):
        return jnp.concatenate([x[:, PAGE:], x[:, :PAGE]], axis=1)

    def send(g):
        peer = pl.ds(g * GROUP, GROUP)
        return pltpu.make_async_copy(stage_ref.at[peer], out_hbm.at[peer], out_sems.at[g])

    for r in range(peers):
        first = table_ref[r, 0]
        second = table_ref[r, 1]
        first, second = (
            jnp.where(first > 0, first - 1, jnp.where(second > 0, second - 2, 0)),
            jnp.where(second > 0, second - 1, jnp.where(first > 0, first, 1)),
        )
        straight = (first % 2 == 0) & (second % 2 == 1)
        beside = straight & (first + 1 == second)

        @pl.when(beside)
        def _(r=r, first=first):
            stage_ref[r] = tile(first)

        @pl.when(straight & jnp.logical_not(beside))
        def _(r=r, first=first, second=second):
            stage_ref[r] = jnp.where(left, tile(first), tile(second))

        @pl.when(jnp.logical_not(straight))
        def _(r=r, first=first, second=second):
            a, b = tile(first), tile(second)
            a = jnp.where(first % 2 == 0, a, turned(a))
            b = jnp.where(second % 2 == 1, b, turned(b))
            stage_ref[r] = jnp.where(left, a, b)

        if r % GROUP == GROUP - 1:
            send(r // GROUP).start()
    for g in range(peers // GROUP):
        send(g).wait()


def pack_pages(table, cache):
    peers = table.shape[0]
    return pl.pallas_call(
        pack_kernel,
        in_specs=[
            pl.BlockSpec(memory_space=pltpu.SMEM),
            pl.BlockSpec(memory_space=pltpu.VMEM),
        ],
        out_specs=pl.BlockSpec(memory_space=pltpu.HBM),
        out_shape=pltpu.HBM((peers, DK, LANES), cache.dtype),
        scratch_shapes=[
            pltpu.VMEM((peers, DK, LANES), cache.dtype),
            pltpu.SemaphoreType.DMA((peers // GROUP,)),
        ],
        compiler_params=pltpu.CompilerParams(vmem_limit_bytes=24 * MIB),
        cost_estimate=pl.CostEstimate(flops=0, bytes_accessed=8 * MIB, transcendentals=0),
        name="pack_pages",
    )(table, cache)


def partner_kernel(place_ref, got_ref, other_ref, *out_refs):
    peers, part = got_ref.shape[0], got_ref.shape[1] - 1
    weights = got_ref[:, part].astype(jnp.float32)
    place = lax.broadcasted_iota(jnp.int32, weights.shape, 1)
    for d, out_ref in enumerate(out_refs):
        row = place_ref[0] ^ d
        mine = row // part == place_ref[1]

        @pl.when(mine)
        def _(out_ref=out_ref, row=row):
            out_ref[:peers] = got_ref[:, row % part]

        @pl.when(jnp.logical_not(mine))
        def _(out_ref=out_ref, row=row):
            out_ref[:peers] = other_ref[:, row % part]

        weight = jnp.sum(jnp.where(place == row, weights, 0.0), axis=1)
        out_ref[peers:] = weight.reshape(peers // 8, 8, LANES).astype(out_ref.dtype)


def partner_parts(place, got, other, rows):
    peers, _, heads, _ = got.shape
    part = jax.ShapeDtypeStruct((peers + peers // 8, heads, LANES), got.dtype)
    return pl.pallas_call(
        partner_kernel,
        in_specs=[
            pl.BlockSpec(memory_space=pltpu.SMEM),
            pl.BlockSpec(memory_space=pltpu.VMEM),
            pl.BlockSpec(memory_space=pltpu.VMEM),
        ],
        out_shape=(part,) * rows,
        compiler_params=pltpu.CompilerParams(vmem_limit_bytes=16 * MIB),
        cost_estimate=pl.CostEstimate(flops=0, bytes_accessed=2 * MIB, transcendentals=0),
        name="partner_parts",
    )(place, got, other)


def score_kernel(key_ref, *refs):
    part_refs, (out_ref, sum_ref) = refs[:-2], refs[-2:]
    step = pl.program_id(0)
    sources = out_ref.shape[0]
    peers = part_refs[0].shape[0] // 9 * 8
    blocks = key_ref.shape[0] // LANES
    heads = part_refs[0].shape[1]
    flat = heads * len(part_refs)
    queries = jnp.concatenate(
        [ref[step * sources + i] for i in range(sources) for ref in part_refs], axis=0
    )
    corner = lax.broadcasted_iota(jnp.int32, (heads, LANES), 0) == lax.broadcasted_iota(
        jnp.int32, (heads, LANES), 1
    )
    tails = [ref[peers + step // 2].astype(jnp.float32) for ref in part_refs]
    half = step % 2 == 0
    weights = []
    for i in range(sources):
        for tail in tails:
            row = jnp.where(half, tail[i : i + 1], tail[sources + i : sources + i + 1])
            column = jnp.sum(jnp.where(corner, row, 0.0), axis=1, keepdims=True)
            weights.append(jnp.broadcast_to(column, (heads, LANES)))
    for b in range(blocks // 2):
        keys = key_ref[2 * b * LANES : 2 * (b + 1) * LANES, :]
        dots = lax.dot_general(
            queries, keys, (((1,), (1,)), ((), ())), preferred_element_type=jnp.float32
        )
        for j in range(2):
            for i in range(sources):
                total = None
                for d in range(len(part_refs)):
                    at = i * flat + d * heads
                    part = (
                        jnp.maximum(dots[at : at + heads, j * LANES : (j + 1) * LANES], 0.0)
                        * weights[i * len(part_refs) + d]
                    )
                    total = part if total is None else total + part
                sum_ref[i, 2 * b + j : 2 * b + j + 1, :] = jnp.sum(total, axis=0, keepdims=True)
    for i in range(sources):
        out_ref[i] = sum_ref[i].astype(out_ref.dtype)


def index_scores(keys, parts):
    sources = 4
    peers = parts[0].shape[0] // 9 * 8
    blocks = keys.shape[0] // LANES
    return pl.pallas_call(
        score_kernel,
        grid=(peers // sources,),
        in_specs=[pl.BlockSpec(memory_space=pltpu.VMEM)] * (1 + len(parts)),
        out_specs=pl.BlockSpec((sources, blocks, LANES), lambda i: (i, 0, 0)),
        out_shape=jax.ShapeDtypeStruct((peers, blocks, LANES), jnp.bfloat16),
        scratch_shapes=[pltpu.VMEM((sources, blocks, LANES), jnp.float32)],
        compiler_params=pltpu.CompilerParams(vmem_limit_bytes=16 * MIB),
        cost_estimate=pl.CostEstimate(
            flops=2 * peers * H_IDX * keys.shape[0] * D_IDX,
            bytes_accessed=2 * MIB,
            transcendentals=0,
        ),
        name="index_scores",
    )(keys, *parts)


def logp_kernel(score_ref, out_ref):
    scores = score_ref[...].astype(jnp.float32)
    top = jnp.max(scores)
    total = jnp.sum(jnp.exp(scores - top), keepdims=True)
    out_ref[...] = scores - (top + jnp.log(total)) + jnp.log(jnp.float32(scores.size))


def log_distribution(scores):
    return pl.pallas_call(
        logp_kernel,
        out_shape=jax.ShapeDtypeStruct(scores.shape, jnp.float32),
        compiler_params=pltpu.CompilerParams(vmem_limit_bytes=8 * MIB),
        cost_estimate=pl.CostEstimate(
            flops=4 * scores.size, bytes_accessed=6 * scores.size, transcendentals=scores.size
        ),
        name="log_distribution",
    )(scores)


def attend_kernel(used_ref, query_ref, page_ref, out_ref, top_ref, total_ref, sum_ref):
    step = pl.program_id(0)
    sources = page_ref.shape[0]

    @pl.when(step == 0)
    def _():
        top_ref[...] = jnp.full_like(top_ref, NEG)
        total_ref[...] = jnp.zeros_like(total_ref)
        sum_ref[...] = jnp.zeros_like(sum_ref)

    left = lax.broadcasted_iota(jnp.int32, (1, LANES), 1) < PAGE
    live = []
    for i in range(sources):
        slots = [
            jnp.where(used_ref[step * sources + i, 0, s] > 0, 0.0, NEG) for s in range(2)
        ]
        live.append(jnp.where(left, slots[0], slots[1]))
    live = jnp.concatenate(live, axis=1)
    keys = jnp.concatenate([page_ref[i] for i in range(sources)], axis=1)
    scale = (QK_NOPE + D_ROPE) ** (-0.5)
    logits = jnp.dot(query_ref[...], keys, preferred_element_type=jnp.float32) * scale + live
    old = top_ref[...]
    new = jnp.maximum(old, jnp.max(logits, axis=1, keepdims=True))
    fade = jnp.exp(old - new)
    top_ref[...] = new
    expo = jnp.exp(logits - new[:, :1])
    total_ref[...] = total_ref[...] * fade + jnp.sum(expo, axis=1, keepdims=True)
    mixed = lax.dot_general(
        expo.astype(jnp.bfloat16),
        keys[:D_LAT],
        (((1,), (1,)), ((), ())),
        preferred_element_type=jnp.float32,
    )
    sum_ref[...] = sum_ref[...] * fade[:, :1] + mixed

    @pl.when(step == pl.num_programs(0) - 1)
    def _():
        out_ref[...] = (sum_ref[...] / total_ref[...][:, :1]).astype(out_ref.dtype)


def attend(used, query, pages):
    sources = 16
    peers = pages.shape[0]
    tokens = peers * LANES
    return pl.pallas_call(
        attend_kernel,
        grid=(peers // sources,),
        in_specs=[
            pl.BlockSpec(memory_space=pltpu.SMEM),
            pl.BlockSpec(memory_space=pltpu.VMEM),
            pl.BlockSpec((sources, DK, LANES), lambda i: (i, 0, 0)),
        ],
        out_specs=pl.BlockSpec((H, D_LAT), lambda i: (0, 0)),
        scratch_shapes=[
            pltpu.VMEM((H, LANES), jnp.float32),
            pltpu.VMEM((H, LANES), jnp.float32),
            pltpu.VMEM((H, D_LAT), jnp.float32),
        ],
        out_shape=jax.ShapeDtypeStruct((H, D_LAT), jnp.bfloat16),
        compiler_params=pltpu.CompilerParams(vmem_limit_bytes=40 * MIB),
        cost_estimate=pl.CostEstimate(
            flops=2 * H * tokens * (2 * D_LAT + D_ROPE),
            bytes_accessed=5 * MIB,
            transcendentals=H * tokens,
        ),
        name="attend",
    )(used, query, pages)


def per_device(idx_query, idx_weight, idx_keys, q_latent, latent_cache, page_ids):
    owners = lax.axis_size("ctx")
    groups = lax.axis_size("qry")
    rows = idx_weight.shape[0]
    exchange = functools.partial(
        lax.all_to_all, axis_name="ctx", split_axis=0, concat_axis=0, tiled=True
    )

    def swap(x, axis, size, bits):
        return lax.ppermute(x, axis, [(i, i ^ bits) for i in range(size)])

    sent, table = requests(page_ids, idx_query, idx_weight, owners, idx_keys.shape[0] // PAGE)
    got, latent, cache = lax.optimization_barrier(
        (exchange(sent), q_latent.reshape(H, DK), stage(latent_cache.T))
    )
    heads = idx_weight.shape[1]
    asked = got[:, rows // 2, 0, heads : heads + 2].astype(jnp.int32)
    packed, got = lax.optimization_barrier((pack_pages(asked, cache), got))
    pages = exchange(packed)

    place = jnp.stack([lax.axis_index("qry"), lax.axis_index("ctx") % 2]).astype(jnp.int32)
    parts = partner_parts(place, got, swap(got, "ctx", owners, 1), rows)
    parts = [parts[0]] + [swap(parts[d], "qry", groups, d) for d in range(1, groups)]
    scores = index_scores(idx_keys, parts)
    scores, pages = lax.optimization_barrier((scores, pages))
    scores = exchange(scores)

    latent_out = attend(table, latent, pages)
    index_logp = log_distribution(scores.reshape(-1, LANES))
    return (index_logp.reshape(1, -1), latent_out.reshape(1, -1))


def solution(mesh):
    in_specs = (
        P("ctx", "qry"),
        P("ctx", "qry"),
        P("ctx", None),
        P(("ctx", "qry"), None),
        P("ctx", None),
        P(("ctx", "qry"), None),
    )
    out_specs = (P(("ctx", "qry"), None), P(("ctx", "qry"), None))
    return jax.shard_map(
        per_device, mesh=mesh, in_specs=in_specs, out_specs=out_specs, check_vma=False
    )
```

```python
import functools

import jax
import jax.numpy as jnp
from jax import lax
from jax.experimental import pallas as pl
from jax.experimental.pallas import tpu as pltpu
from jax.sharding import PartitionSpec as P

H_IDX = 64
D_IDX = 128
H = 128
D_LAT = 512
D_ROPE = 64
DK = D_LAT + D_ROPE
QK_NOPE = 128
PAGE = 64
TOPP = 32
LANES = 128
CORES = 2
NEG = -1e30
MIB = 1 << 20


def request_kernel(pages_dev, ids_ref, query_ref, weight_ref, out_ref, table_ref, turn_ref):
    owners = table_ref.shape[0]
    rows, heads = weight_ref.shape
    ids = ids_ref[...]
    owner, local = ids // pages_dev, ids % pages_dev
    mine = owner == lax.broadcasted_iota(jnp.int32, (owners, TOPP), 0)
    low = jnp.min(jnp.where(mine, local, pages_dev), axis=1, keepdims=True)
    high = jnp.max(jnp.where(mine, local, -1), axis=1, keepdims=True)
    turn = (low < high) & (low % 2 == 1) & (high % 2 == 0)
    first = jnp.where(turn, high, low)
    second = jnp.where(turn, low, high)
    single = low == high
    left = jnp.where((high < 0) | (single & (low % 2 == 1)), 0, first + 1)
    right = jnp.where((high < 0) | (single & (low % 2 == 0)), 0, second + 1)
    lane = lax.broadcasted_iota(jnp.int32, (owners, LANES), 1)
    table = jnp.where(lane == 0, left, jnp.where(lane == 1, right, 0)).reshape(owners, 1, LANES)
    table_ref[...] = table
    weight = jnp.concatenate(
        [weight_ref[...].astype(jnp.float32), jnp.zeros((rows, LANES - heads), jnp.float32)], axis=1
    )
    pair = table.reshape(owners // CORES, CORES, LANES).astype(jnp.float32)
    lane = lax.broadcasted_iota(jnp.int32, (owners // CORES, LANES), 1)
    asked = jnp.zeros((owners // CORES, LANES), jnp.float32)
    for core in range(CORES):
        for s in range(2):
            asked = jnp.where(lane == heads + 2 * core + s, pair[:, core, s : s + 1], asked)
    for h in range(heads):
        turn_ref[pl.ds(h, rows, stride=heads), :] = query_ref[
            :, h * LANES : (h + 1) * LANES
        ].astype(jnp.float32)
    query = turn_ref[...].astype(out_ref.dtype).reshape(rows, heads, LANES)
    out_ref[:, :rows] = jnp.broadcast_to(query[None], (owners // CORES, rows, heads, LANES))
    out_ref[:, rows] = (weight[None] + asked[:, None]).astype(out_ref.dtype)


def requests(page_ids, query, weight, owners, pages_dev):
    rows, heads = weight.shape
    return pl.pallas_call(
        functools.partial(request_kernel, pages_dev),
        out_shape=(
            pltpu.HBM((owners // CORES, rows + 1, heads, LANES), query.dtype),
            jax.ShapeDtypeStruct((owners, 1, LANES), jnp.int32),
        ),
        scratch_shapes=[pltpu.VMEM((rows * heads, LANES), jnp.float32)],
        name="requests",
    )(page_ids, query, weight)


def stage_kernel(cache_hbm, out_ref, sem):
    load = pltpu.make_async_copy(cache_hbm, out_ref, sem)
    load.start()
    load.wait()


def stage(cache):
    return pl.pallas_call(
        stage_kernel,
        in_specs=[pl.BlockSpec(memory_space=pltpu.HBM)],
        out_specs=pl.BlockSpec(memory_space=pltpu.VMEM),
        out_shape=pltpu.VMEM(cache.shape, cache.dtype),
        scratch_shapes=[pltpu.SemaphoreType.DMA],
        compiler_params=pltpu.CompilerParams(vmem_limit_bytes=60 * MIB),
        cost_estimate=pl.CostEstimate(flops=0, bytes_accessed=5 * MIB, transcendentals=0),
        name="stage",
    )(cache)


def pack_kernel(place_ref, table_ref, own_ref, other_hbm, out_hbm, other_ref, stage_ref, in_sem, out_sems):
    peers = table_ref.shape[0]
    load = pltpu.make_async_copy(other_hbm, other_ref, in_sem)
    load.start()
    left = lax.broadcasted_iota(jnp.int32, (DK, LANES), 1) < PAGE

    def turned(x):
        return jnp.concatenate([x[:, PAGE:], x[:, :PAGE]], axis=1)

    def send(at, block):
        return pltpu.make_async_copy(stage_ref.at[at], out_hbm.at[block], out_sems.at[at])

    def pack(at, block, cache_ref, first, second):
        def tile(page):
            return cache_ref[:, pl.ds(pl.multiple_of(page // 2 * LANES, LANES), LANES)]

        first, second = (
            jnp.where(first > 0, first - 1, jnp.where(second > 0, second - 2, 0)),
            jnp.where(second > 0, second - 1, jnp.where(first > 0, first, 1)),
        )
        straight = (first % 2 == 0) & (second % 2 == 1)
        beside = straight & (first + 1 == second)

        @pl.when(beside)
        def _():
            stage_ref[at] = tile(first)

        @pl.when(straight & jnp.logical_not(beside))
        def _():
            stage_ref[at] = jnp.where(left, tile(first), tile(second))

        @pl.when(jnp.logical_not(straight))
        def _():
            a, b = tile(first), tile(second)
            a = jnp.where(first % 2 == 0, a, turned(a))
            b = jnp.where(second % 2 == 1, b, turned(b))
            stage_ref[at] = jnp.where(left, a, b)

        send(at, block).start()

    own = place_ref[1]
    for half, (cache_ref, core) in enumerate(((own_ref, own), (other_ref, 1 - own))):
        if half == 1:
            load.wait()
        for r in range(peers):
            pack(
                half * peers + r,
                CORES * r + core,
                cache_ref,
                table_ref[r, 2 * core],
                table_ref[r, 2 * core + 1],
            )
    for half, core in enumerate((own, 1 - own)):
        for r in range(peers):
            send(half * peers + r, CORES * r + core).wait()


def pack_pages(place, table, own, other):
    blocks = table.shape[0] * CORES
    return pl.pallas_call(
        pack_kernel,
        in_specs=[
            pl.BlockSpec(memory_space=pltpu.SMEM),
            pl.BlockSpec(memory_space=pltpu.SMEM),
            pl.BlockSpec(memory_space=pltpu.VMEM),
            pl.BlockSpec(memory_space=pltpu.HBM),
        ],
        out_specs=pl.BlockSpec(memory_space=pltpu.HBM),
        out_shape=pltpu.HBM((blocks, DK, LANES), own.dtype),
        scratch_shapes=[
            pltpu.VMEM(own.shape, own.dtype),
            pltpu.VMEM((blocks, DK, LANES), own.dtype),
            pltpu.SemaphoreType.DMA,
            pltpu.SemaphoreType.DMA((blocks,)),
        ],
        compiler_params=pltpu.CompilerParams(vmem_limit_bytes=50 * MIB),
        cost_estimate=pl.CostEstimate(flops=0, bytes_accessed=8 * MIB, transcendentals=0),
        name="pack_pages",
    )(place, table, own, other)


def partner_kernel(place_ref, got_ref, *out_refs):
    peers = got_ref.shape[0]
    rows = len(out_refs)
    weights = got_ref[:, rows].astype(jnp.float32)
    place = lax.broadcasted_iota(jnp.int32, weights.shape, 1)
    for d, out_ref in enumerate(out_refs):
        row = place_ref[0] ^ d
        out_ref[:peers] = got_ref[:, row]
        weight = jnp.sum(jnp.where(place == row, weights, 0.0), axis=1)
        out_ref[peers:] = weight.reshape(peers // 8, 8, LANES).astype(out_ref.dtype)


def partner_parts(place, got, rows):
    peers, _, heads, _ = got.shape
    part = jax.ShapeDtypeStruct((peers + peers // 8, heads, LANES), got.dtype)
    return pl.pallas_call(
        partner_kernel,
        in_specs=[
            pl.BlockSpec(memory_space=pltpu.SMEM),
            pl.BlockSpec(memory_space=pltpu.VMEM),
        ],
        out_shape=(part,) * rows,
        compiler_params=pltpu.CompilerParams(vmem_limit_bytes=16 * MIB),
        cost_estimate=pl.CostEstimate(flops=0, bytes_accessed=2 * MIB, transcendentals=0),
        name="partner_parts",
    )(place, got)


def score_kernel(key_ref, *refs):
    part_refs, (out_ref, sum_ref) = refs[:-2], refs[-2:]
    step = pl.program_id(0)
    sources = out_ref.shape[0]
    peers = part_refs[0].shape[0] // 9 * 8
    blocks = key_ref.shape[0] // LANES
    heads = part_refs[0].shape[1]
    flat = heads * len(part_refs)
    queries = jnp.concatenate(
        [ref[step * sources + i] for i in range(sources) for ref in part_refs], axis=0
    )
    corner = lax.broadcasted_iota(jnp.int32, (heads, LANES), 0) == lax.broadcasted_iota(
        jnp.int32, (heads, LANES), 1
    )
    tails = [ref[peers + step // 2].astype(jnp.float32) for ref in part_refs]
    half = step % 2 == 0
    weights = []
    for i in range(sources):
        for tail in tails:
            row = jnp.where(half, tail[i : i + 1], tail[sources + i : sources + i + 1])
            column = jnp.sum(jnp.where(corner, row, 0.0), axis=1, keepdims=True)
            weights.append(jnp.broadcast_to(column, (heads, LANES)))
    for b in range(blocks // 2):
        keys = key_ref[2 * b * LANES : 2 * (b + 1) * LANES, :]
        dots = lax.dot_general(
            queries, keys, (((1,), (1,)), ((), ())), preferred_element_type=jnp.float32
        )
        for j in range(2):
            for i in range(sources):
                total = None
                for d in range(len(part_refs)):
                    at = i * flat + d * heads
                    part = (
                        jnp.maximum(dots[at : at + heads, j * LANES : (j + 1) * LANES], 0.0)
                        * weights[i * len(part_refs) + d]
                    )
                    total = part if total is None else total + part
                sum_ref[i, 2 * b + j : 2 * b + j + 1, :] = jnp.sum(total, axis=0, keepdims=True)
    for i in range(sources):
        out_ref[i] = sum_ref[i].astype(out_ref.dtype)


def index_scores(keys, parts):
    sources = 4
    peers = parts[0].shape[0] // 9 * 8
    blocks = keys.shape[0] // LANES
    return pl.pallas_call(
        score_kernel,
        grid=(peers // sources,),
        in_specs=[pl.BlockSpec(memory_space=pltpu.VMEM)] * (1 + len(parts)),
        out_specs=pl.BlockSpec((sources, blocks, LANES), lambda i: (i, 0, 0)),
        out_shape=jax.ShapeDtypeStruct((peers, blocks, LANES), jnp.bfloat16),
        scratch_shapes=[pltpu.VMEM((sources, blocks, LANES), jnp.float32)],
        compiler_params=pltpu.CompilerParams(vmem_limit_bytes=16 * MIB),
        cost_estimate=pl.CostEstimate(
            flops=2 * peers * H_IDX * keys.shape[0] * D_IDX,
            bytes_accessed=2 * MIB,
            transcendentals=0,
        ),
        name="index_scores",
    )(keys, *parts)


def logp_kernel(score_ref, out_ref):
    scores = score_ref[...].astype(jnp.float32)
    top = jnp.max(scores)
    total = jnp.sum(jnp.exp(scores - top), keepdims=True)
    out_ref[...] = scores - (top + jnp.log(total)) + jnp.log(jnp.float32(scores.size))


def log_distribution(scores):
    return pl.pallas_call(
        logp_kernel,
        out_shape=jax.ShapeDtypeStruct(scores.shape, jnp.float32),
        compiler_params=pltpu.CompilerParams(vmem_limit_bytes=8 * MIB),
        cost_estimate=pl.CostEstimate(
            flops=4 * scores.size, bytes_accessed=6 * scores.size, transcendentals=scores.size
        ),
        name="log_distribution",
    )(scores)


def attend_kernel(used_ref, query_ref, page_ref, out_ref, top_ref, total_ref, sum_ref):
    step = pl.program_id(0)
    sources = page_ref.shape[0]

    @pl.when(step == 0)
    def _():
        top_ref[...] = jnp.full_like(top_ref, NEG)
        total_ref[...] = jnp.zeros_like(total_ref)
        sum_ref[...] = jnp.zeros_like(sum_ref)

    left = lax.broadcasted_iota(jnp.int32, (1, LANES), 1) < PAGE
    live = []
    for i in range(sources):
        slots = [
            jnp.where(used_ref[step * sources + i, 0, s] > 0, 0.0, NEG) for s in range(2)
        ]
        live.append(jnp.where(left, slots[0], slots[1]))
    live = jnp.concatenate(live, axis=1)
    keys = jnp.concatenate([page_ref[i] for i in range(sources)], axis=1)
    scale = (QK_NOPE + D_ROPE) ** (-0.5)
    logits = jnp.dot(query_ref[...], keys, preferred_element_type=jnp.float32) * scale + live
    old = top_ref[...]
    new = jnp.maximum(old, jnp.max(logits, axis=1, keepdims=True))
    fade = jnp.exp(old - new)
    top_ref[...] = new
    expo = jnp.exp(logits - new[:, :1])
    total_ref[...] = total_ref[...] * fade + jnp.sum(expo, axis=1, keepdims=True)
    mixed = lax.dot_general(
        expo.astype(jnp.bfloat16),
        keys[:D_LAT],
        (((1,), (1,)), ((), ())),
        preferred_element_type=jnp.float32,
    )
    sum_ref[...] = sum_ref[...] * fade[:, :1] + mixed

    @pl.when(step == pl.num_programs(0) - 1)
    def _():
        out_ref[...] = (sum_ref[...] / total_ref[...][:, :1]).astype(out_ref.dtype)


def attend(used, query, pages):
    sources = 16
    peers = pages.shape[0]
    tokens = peers * LANES
    return pl.pallas_call(
        attend_kernel,
        grid=(peers // sources,),
        in_specs=[
            pl.BlockSpec(memory_space=pltpu.SMEM),
            pl.BlockSpec(memory_space=pltpu.VMEM),
            pl.BlockSpec((sources, DK, LANES), lambda i: (i, 0, 0)),
        ],
        out_specs=pl.BlockSpec((H, D_LAT), lambda i: (0, 0)),
        scratch_shapes=[
            pltpu.VMEM((H, LANES), jnp.float32),
            pltpu.VMEM((H, LANES), jnp.float32),
            pltpu.VMEM((H, D_LAT), jnp.float32),
        ],
        out_shape=jax.ShapeDtypeStruct((H, D_LAT), jnp.bfloat16),
        compiler_params=pltpu.CompilerParams(vmem_limit_bytes=40 * MIB),
        cost_estimate=pl.CostEstimate(
            flops=2 * H * tokens * (2 * D_LAT + D_ROPE),
            bytes_accessed=5 * MIB,
            transcendentals=H * tokens,
        ),
        name="attend",
    )(used, query, pages)


def per_device(idx_query, idx_weight, idx_keys, q_latent, latent_cache, page_ids):
    owners = lax.axis_size("ctx")
    groups = lax.axis_size("qry")
    rows = idx_weight.shape[0]
    same_core = [list(range(core, owners, CORES)) for core in range(CORES)]
    exchange = functools.partial(
        lax.all_to_all,
        axis_name="ctx",
        split_axis=0,
        concat_axis=0,
        axis_index_groups=same_core,
        tiled=True,
    )

    def swap(x, axis, size, bits):
        return lax.ppermute(x, axis, [(i, i ^ bits) for i in range(size)])

    core = lax.axis_index("ctx") & 1
    place = jnp.stack([lax.axis_index("qry"), core]).astype(jnp.int32)
    sent, table = requests(page_ids, idx_query, idx_weight, owners, idx_keys.shape[0] // PAGE)
    cache = latent_cache.T
    other = swap(cache, "ctx", owners, 1)
    got, latent, cache, other = lax.optimization_barrier(
        (exchange(sent), q_latent.reshape(H, DK), stage(cache), other)
    )
    heads = idx_weight.shape[1]
    asked = got[:, rows, 0, heads : heads + 2 * CORES].astype(jnp.int32)
    packed, got = lax.optimization_barrier((pack_pages(place, asked, cache, other), got))
    pages = exchange(packed)

    other_keys = swap(idx_keys, "ctx", owners, 1)
    keys = jnp.where(
        core == 0,
        jnp.concatenate([idx_keys, other_keys], axis=0),
        jnp.concatenate([other_keys, idx_keys], axis=0),
    )
    parts = partner_parts(place, got, rows)
    parts = [parts[0]] + [swap(parts[d], "qry", groups, d) for d in range(1, groups)]
    scores = index_scores(keys, parts)
    scores, pages = lax.optimization_barrier((scores, pages))
    scores = exchange(scores)

    latent_out = attend(table, latent, pages)
    index_logp = log_distribution(scores.reshape(-1, LANES))
    return (index_logp.reshape(1, -1), latent_out.reshape(1, -1))


def solution(mesh):
    in_specs = (
        P("ctx", "qry"),
        P("ctx", "qry"),
        P("ctx", None),
        P(("ctx", "qry"), None),
        P("ctx", None),
        P(("ctx", "qry"), None),
    )
    out_specs = (P(("ctx", "qry"), None), P(("ctx", "qry"), None))
    return jax.shard_map(
        per_device, mesh=mesh, in_specs=in_specs, out_specs=out_specs, check_vma=False
    )
```

```python
import functools

import jax
import jax.numpy as jnp
from jax import lax
from jax.experimental import pallas as pl
from jax.experimental.pallas import tpu as pltpu
from jax.sharding import PartitionSpec as P

H_IDX = 64
D_IDX = 128
H = 128
D_LAT = 512
D_ROPE = 64
DK = D_LAT + D_ROPE
QK_NOPE = 128
PAGE = 64
TOPP = 32
LANES = 128
NEG = -1e30
MIB = 1 << 20


def request_kernel(pages_dev, ids_ref, query_ref, weight_ref, out_ref, table_ref, turn_ref):
    owners = out_ref.shape[0]
    rows, heads = weight_ref.shape
    part = rows // 2
    ids = ids_ref[...]
    owner, local = ids // pages_dev, ids % pages_dev
    mine = owner == lax.broadcasted_iota(jnp.int32, (owners, TOPP), 0)
    low = jnp.min(jnp.where(mine, local, pages_dev), axis=1, keepdims=True)
    high = jnp.max(jnp.where(mine, local, -1), axis=1, keepdims=True)
    turn = (low < high) & (low % 2 == 1) & (high % 2 == 0)
    first = jnp.where(turn, high, low)
    second = jnp.where(turn, low, high)
    single = low == high
    left = jnp.where((high < 0) | (single & (low % 2 == 1)), 0, first + 1)
    right = jnp.where((high < 0) | (single & (low % 2 == 0)), 0, second + 1)
    lane = lax.broadcasted_iota(jnp.int32, (owners, LANES), 1)
    table = jnp.where(lane == 0, left, jnp.where(lane == 1, right, 0)).reshape(owners, 1, LANES)
    table_ref[...] = table
    weight = jnp.concatenate(
        [weight_ref[...].astype(jnp.float32), jnp.zeros((rows, LANES - heads), jnp.float32)], axis=1
    )
    asked = jnp.where(lane == heads, left, jnp.where(lane == heads + 1, right, 0))
    asked = asked.astype(jnp.float32).reshape(owners, 1, LANES)
    for h in range(heads):
        turn_ref[pl.ds(h, rows, stride=heads), :] = query_ref[
            :, h * LANES : (h + 1) * LANES
        ].astype(jnp.float32)
    query = turn_ref[...].astype(out_ref.dtype).reshape(rows, heads, LANES)
    for t in range(owners):
        out_ref[t, :part] = query[t % 2 * part : (t % 2 + 1) * part]
    out_ref[:, part] = (weight[None] + asked).astype(out_ref.dtype)


def requests(page_ids, query, weight, owners, pages_dev):
    rows, heads = weight.shape
    return pl.pallas_call(
        functools.partial(request_kernel, pages_dev),
        out_shape=(
            pltpu.HBM((owners, rows // 2 + 1, heads, LANES), query.dtype),
            jax.ShapeDtypeStruct((owners, 1, LANES), jnp.int32),
        ),
        scratch_shapes=[pltpu.VMEM((rows * heads, LANES), jnp.float32)],
        name="requests",
    )(page_ids, query, weight)


def stage_kernel(cache_hbm, out_ref, sem):
    load = pltpu.make_async_copy(cache_hbm, out_ref, sem)
    load.start()
    load.wait()


def stage(cache):
    return pl.pallas_call(
        stage_kernel,
        in_specs=[pl.BlockSpec(memory_space=pltpu.HBM)],
        out_specs=pl.BlockSpec(memory_space=pltpu.VMEM),
        out_shape=pltpu.VMEM(cache.shape, cache.dtype),
        scratch_shapes=[pltpu.SemaphoreType.DMA],
        compiler_params=pltpu.CompilerParams(vmem_limit_bytes=60 * MIB),
        cost_estimate=pl.CostEstimate(flops=0, bytes_accessed=5 * MIB, transcendentals=0),
        name="stage",
    )(cache)


GROUP = 4


def pack_kernel(table_ref, cache_ref, out_hbm, stage_ref, out_sems):
    peers = stage_ref.shape[0]
    left = lax.broadcasted_iota(jnp.int32, (DK, LANES), 1) < PAGE

    def tile(page):
        return cache_ref[:, pl.ds(pl.multiple_of(page // 2 * LANES, LANES), LANES)]

    def turned(x):
        return jnp.concatenate([x[:, PAGE:], x[:, :PAGE]], axis=1)

    def send(g):
        peer = pl.ds(g * GROUP, GROUP)
        return pltpu.make_async_copy(stage_ref.at[peer], out_hbm.at[peer], out_sems.at[g])

    for r in range(peers):
        first = table_ref[r, 0]
        second = table_ref[r, 1]
        first, second = (
            jnp.where(first > 0, first - 1, jnp.where(second > 0, second - 2, 0)),
            jnp.where(second > 0, second - 1, jnp.where(first > 0, first, 1)),
        )
        straight = (first % 2 == 0) & (second % 2 == 1)
        beside = straight & (first + 1 == second)

        @pl.when(beside)
        def _(r=r, first=first):
            stage_ref[r] = tile(first)

        @pl.when(straight & jnp.logical_not(beside))
        def _(r=r, first=first, second=second):
            stage_ref[r] = jnp.where(left, tile(first), tile(second))

        @pl.when(jnp.logical_not(straight))
        def _(r=r, first=first, second=second):
            a, b = tile(first), tile(second)
            a = jnp.where(first % 2 == 0, a, turned(a))
            b = jnp.where(second % 2 == 1, b, turned(b))
            stage_ref[r] = jnp.where(left, a, b)

        if r % GROUP == GROUP - 1:
            send(r // GROUP).start()
    for g in range(peers // GROUP):
        send(g).wait()


def pack_pages(table, cache):
    peers = table.shape[0]
    return pl.pallas_call(
        pack_kernel,
        in_specs=[
            pl.BlockSpec(memory_space=pltpu.SMEM),
            pl.BlockSpec(memory_space=pltpu.VMEM),
        ],
        out_specs=pl.BlockSpec(memory_space=pltpu.HBM),
        out_shape=pltpu.HBM((peers, DK, LANES), cache.dtype),
        scratch_shapes=[
            pltpu.VMEM((peers, DK, LANES), cache.dtype),
            pltpu.SemaphoreType.DMA((peers // GROUP,)),
        ],
        compiler_params=pltpu.CompilerParams(vmem_limit_bytes=24 * MIB),
        cost_estimate=pl.CostEstimate(flops=0, bytes_accessed=8 * MIB, transcendentals=0),
        name="pack_pages",
    )(table, cache)


def partner_kernel(place_ref, got_ref, other_ref, *out_refs):
    peers, part = got_ref.shape[0], got_ref.shape[1] - 1
    weights = got_ref[:, part].astype(jnp.float32)
    place = lax.broadcasted_iota(jnp.int32, weights.shape, 1)
    for d, out_ref in enumerate(out_refs):
        row = place_ref[0] ^ d
        mine = row // part == place_ref[1]

        @pl.when(mine)
        def _(out_ref=out_ref, row=row):
            out_ref[:peers] = got_ref[:, row % part]

        @pl.when(jnp.logical_not(mine))
        def _(out_ref=out_ref, row=row):
            out_ref[:peers] = other_ref[:, row % part]

        weight = jnp.sum(jnp.where(place == row, weights, 0.0), axis=1)
        out_ref[peers:] = weight.reshape(peers // 8, 8, LANES).astype(out_ref.dtype)


def partner_parts(place, got, other, rows):
    peers, _, heads, _ = got.shape
    part = jax.ShapeDtypeStruct((peers + peers // 8, heads, LANES), got.dtype)
    return pl.pallas_call(
        partner_kernel,
        in_specs=[
            pl.BlockSpec(memory_space=pltpu.SMEM),
            pl.BlockSpec(memory_space=pltpu.VMEM),
            pl.BlockSpec(memory_space=pltpu.VMEM),
        ],
        out_shape=(part,) * rows,
        compiler_params=pltpu.CompilerParams(vmem_limit_bytes=16 * MIB),
        cost_estimate=pl.CostEstimate(flops=0, bytes_accessed=2 * MIB, transcendentals=0),
        name="partner_parts",
    )(place, got, other)


def score_kernel(key_ref, *refs):
    part_refs, (out_ref, sum_ref) = refs[:-2], refs[-2:]
    step = pl.program_id(0)
    sources = out_ref.shape[0]
    peers = part_refs[0].shape[0] // 9 * 8
    blocks = key_ref.shape[0] // LANES
    heads = part_refs[0].shape[1]
    flat = heads * len(part_refs)
    queries = jnp.concatenate(
        [ref[step * sources + i] for i in range(sources) for ref in part_refs], axis=0
    )
    corner = lax.broadcasted_iota(jnp.int32, (heads, LANES), 0) == lax.broadcasted_iota(
        jnp.int32, (heads, LANES), 1
    )
    tails = [ref[peers + step // 2].astype(jnp.float32) for ref in part_refs]
    half = step % 2 == 0
    weights = []
    for i in range(sources):
        for tail in tails:
            row = jnp.where(half, tail[i : i + 1], tail[sources + i : sources + i + 1])
            column = jnp.sum(jnp.where(corner, row, 0.0), axis=1, keepdims=True)
            weights.append(jnp.broadcast_to(column, (heads, LANES)))
    for b in range(blocks // 2):
        keys = key_ref[2 * b * LANES : 2 * (b + 1) * LANES, :]
        dots = lax.dot_general(
            queries, keys, (((1,), (1,)), ((), ())), preferred_element_type=jnp.float32
        )
        for j in range(2):
            for i in range(sources):
                total = None
                for d in range(len(part_refs)):
                    at = i * flat + d * heads
                    part = (
                        jnp.maximum(dots[at : at + heads, j * LANES : (j + 1) * LANES], 0.0)
                        * weights[i * len(part_refs) + d]
                    )
                    total = part if total is None else total + part
                sum_ref[i, 2 * b + j : 2 * b + j + 1, :] = jnp.sum(total, axis=0, keepdims=True)
    for i in range(sources):
        out_ref[i] = sum_ref[i].astype(out_ref.dtype)


def index_scores(keys, parts):
    sources = 4
    peers = parts[0].shape[0] // 9 * 8
    blocks = keys.shape[0] // LANES
    return pl.pallas_call(
        score_kernel,
        grid=(peers // sources,),
        in_specs=[pl.BlockSpec(memory_space=pltpu.VMEM)] * (1 + len(parts)),
        out_specs=pl.BlockSpec((sources, blocks, LANES), lambda i: (i, 0, 0)),
        out_shape=jax.ShapeDtypeStruct((peers, blocks, LANES), jnp.bfloat16),
        scratch_shapes=[pltpu.VMEM((sources, blocks, LANES), jnp.float32)],
        compiler_params=pltpu.CompilerParams(vmem_limit_bytes=16 * MIB),
        cost_estimate=pl.CostEstimate(
            flops=2 * peers * H_IDX * keys.shape[0] * D_IDX,
            bytes_accessed=2 * MIB,
            transcendentals=0,
        ),
        name="index_scores",
    )(keys, *parts)


def logp_kernel(score_ref, out_ref):
    scores = score_ref[...].astype(jnp.float32)
    top = jnp.max(scores)
    total = jnp.sum(jnp.exp(scores - top), keepdims=True)
    out_ref[...] = scores - (top + jnp.log(total)) + jnp.log(jnp.float32(scores.size))


def log_distribution(scores):
    return pl.pallas_call(
        logp_kernel,
        out_shape=jax.ShapeDtypeStruct(scores.shape, jnp.float32),
        compiler_params=pltpu.CompilerParams(vmem_limit_bytes=8 * MIB),
        cost_estimate=pl.CostEstimate(
            flops=4 * scores.size, bytes_accessed=6 * scores.size, transcendentals=scores.size
        ),
        name="log_distribution",
    )(scores)


def attend_kernel(used_ref, query_ref, page_ref, out_ref, top_ref, total_ref, sum_ref):
    step = pl.program_id(0)
    sources = page_ref.shape[0]

    @pl.when(step == 0)
    def _():
        top_ref[...] = jnp.full_like(top_ref, NEG)
        total_ref[...] = jnp.zeros_like(total_ref)
        sum_ref[...] = jnp.zeros_like(sum_ref)

    left = lax.broadcasted_iota(jnp.int32, (1, LANES), 1) < PAGE
    live = []
    for i in range(sources):
        slots = [
            jnp.where(used_ref[step * sources + i, 0, s] > 0, 0.0, NEG) for s in range(2)
        ]
        live.append(jnp.where(left, slots[0], slots[1]))
    live = jnp.concatenate(live, axis=1)
    keys = jnp.concatenate([page_ref[i] for i in range(sources)], axis=1)
    scale = (QK_NOPE + D_ROPE) ** (-0.5)
    logits = jnp.dot(query_ref[...], keys, preferred_element_type=jnp.float32) * scale + live
    old = top_ref[...]
    new = jnp.maximum(old, jnp.max(logits, axis=1, keepdims=True))
    fade = jnp.exp(old - new)
    top_ref[...] = new
    expo = jnp.exp(logits - new[:, :1])
    total_ref[...] = total_ref[...] * fade + jnp.sum(expo, axis=1, keepdims=True)
    mixed = lax.dot_general(
        expo.astype(jnp.bfloat16),
        keys[:D_LAT],
        (((1,), (1,)), ((), ())),
        preferred_element_type=jnp.float32,
    )
    sum_ref[...] = sum_ref[...] * fade[:, :1] + mixed

    @pl.when(step == pl.num_programs(0) - 1)
    def _():
        sum_ref[...] = sum_ref[...] / total_ref[...][:, :1]
        for h in range(H):
            out_ref[:, h * D_LAT : (h + 1) * D_LAT] = sum_ref[h : h + 1, :].astype(out_ref.dtype)


def attend(used, query, pages):
    sources = 16
    peers = pages.shape[0]
    tokens = peers * LANES
    return pl.pallas_call(
        attend_kernel,
        grid=(peers // sources,),
        in_specs=[
            pl.BlockSpec(memory_space=pltpu.SMEM),
            pl.BlockSpec(memory_space=pltpu.VMEM),
            pl.BlockSpec((sources, DK, LANES), lambda i: (i, 0, 0)),
        ],
        out_specs=pl.BlockSpec((1, H * D_LAT), lambda i: (0, 0)),
        scratch_shapes=[
            pltpu.VMEM((H, LANES), jnp.float32),
            pltpu.VMEM((H, LANES), jnp.float32),
            pltpu.VMEM((H, D_LAT), jnp.float32),
        ],
        out_shape=jax.ShapeDtypeStruct((1, H * D_LAT), jnp.bfloat16),
        compiler_params=pltpu.CompilerParams(vmem_limit_bytes=40 * MIB),
        cost_estimate=pl.CostEstimate(
            flops=2 * H * tokens * (2 * D_LAT + D_ROPE),
            bytes_accessed=5 * MIB,
            transcendentals=H * tokens,
        ),
        name="attend",
    )(used, query, pages)


def per_device(idx_query, idx_weight, idx_keys, q_latent, latent_cache, page_ids):
    owners = lax.axis_size("ctx")
    groups = lax.axis_size("qry")
    rows = idx_weight.shape[0]
    exchange = functools.partial(
        lax.all_to_all, axis_name="ctx", split_axis=0, concat_axis=0, tiled=True
    )

    def swap(x, axis, size, bits):
        return lax.ppermute(x, axis, [(i, i ^ bits) for i in range(size)])

    sent, table = requests(page_ids, idx_query, idx_weight, owners, idx_keys.shape[0] // PAGE)
    got, latent, cache = lax.optimization_barrier(
        (exchange(sent), q_latent.reshape(H, DK), stage(latent_cache.T))
    )
    heads = idx_weight.shape[1]
    asked = got[:, rows // 2, 0, heads : heads + 2].astype(jnp.int32)
    packed, got = lax.optimization_barrier((pack_pages(asked, cache), got))
    pages = exchange(packed)

    place = jnp.stack([lax.axis_index("qry"), lax.axis_index("ctx") % 2]).astype(jnp.int32)
    parts = partner_parts(place, got, swap(got, "ctx", owners, 1), rows)
    parts = [parts[0]] + [swap(parts[d], "qry", groups, d) for d in range(1, groups)]
    scores = index_scores(idx_keys, parts)
    scores, pages = lax.optimization_barrier((scores, pages))
    scores = exchange(scores)

    latent_out = attend(table, latent, pages)
    index_logp = log_distribution(scores.reshape(-1, LANES))
    return (index_logp.reshape(1, -1), latent_out.reshape(1, -1))


def solution(mesh):
    in_specs = (
        P("ctx", "qry"),
        P("ctx", "qry"),
        P("ctx", None),
        P(("ctx", "qry"), None),
        P("ctx", None),
        P(("ctx", "qry"), None),
    )
    out_specs = (P(("ctx", "qry"), None), P(("ctx", "qry"), None))
    return jax.shard_map(
        per_device, mesh=mesh, in_specs=in_specs, out_specs=out_specs, check_vma=False
    )
```
